32 devices in a mesh: dp: 8 (over y, x, core), tensor: 4 (over z).
Axes of the slice: x: 2, y: 2, z: 4, core: 2. Of those that a mesh axis runs over, the one named last changes fastest.
Arguments:
- inputs: bfloat16 [2048, 4096], P(('dp', 'tensor')), may hold values from -6 to 6
- out_grad: bfloat16 [2048, 4096], P(('dp', 'tensor')), may hold values from -0.29882812 to 0.29882812
- gate_act: bfloat16 [2048, 14336], P('dp', 'tensor'), may hold values from -6 to 6
- up_act: bfloat16 [2048, 14336], P('dp', 'tensor'), may hold values from -6 to 6
- w_down: bfloat16 [14336, 4096], P('tensor'), may hold values from -0.046875 to 0.046875
- ranks: int32 [3], replicated, may hold values from 8 to 64, as said below
- token_count: int32 [8], P('dp'), may hold values from 128 to 256, as said below
Outputs:
- p_gate: float32 [4, 64, 4096], P('tensor')
- q_gate: float32 [64, 14336], P(None, 'tensor')
- p_up: float32 [4, 64, 4096], P('tensor')
- q_up: float32 [64, 14336], P(None, 'tensor')
- p_down: float32 [64, 14336], P(None, 'tensor')
- q_down: float32 [4, 64, 4096], P('tensor')
The draws below stay inside these ranges and needn't reach their ends.
Inputs may be any that keep to these rules, and one draw needn't show every extreme that they name: `ranks`: each rank is a multiple of 8; one of the three equals 64 and another 64 / 8. `token_count`: at least one replica has all its tokens live.
All inputs are finite; a program needn't handle non-finite values.
Results may differ from the reference program's by a relative error of at most 0.0063.
Values may be sent and summed in bfloat16 or wider, within the bound.
A program may use at most 128 MiB of HBM per device.

```python
import jax
import jax.numpy as jnp
from jax import lax

D = 4096
FF = 14336
TOK_DEV = 64
RMAX = 64
TOKENS = 2048
N_DP = 8
N_TENSOR = 4


def draw_ranks(key, part):
    key = jax.random.fold_in(key, 11)
    first_key, second_key = jax.random.split(key)
    step_size = RMAX // 8
    values = step_size * jax.random.randint(first_key, (3,), 1, 9)
    order = jax.random.permutation(second_key, 3)
    values = values.at[order[0]].set(RMAX)
    values = values.at[order[1]].set(step_size)
    return values.astype(jnp.int32)


def draw_token_count(key, part):
    key = jax.random.fold_in(key, 23)
    first_key, second_key = jax.random.split(key)
    replica_rows = TOK_DEV * N_TENSOR
    counts = jax.random.randint(first_key, (N_DP,), replica_rows // 2, replica_rows + 1)
    chosen = jax.random.randint(second_key, (), 0, N_DP)
    counts = counts.at[chosen].set(replica_rows)
    return counts.astype(jnp.int32)


def steps_of(key, extent, cuts, low, high):
    def one(dim, parts):
        draws = jax.random.uniform(jax.random.fold_in(jax.random.fold_in(key, 6), dim), (parts,), jnp.float32, low / len(cuts), high / len(cuts))
        return jnp.repeat(jnp.exp(draws), extent[dim] // parts).reshape((-1,) + (1,) * (len(extent) - dim - 1))

    factor_of = one(*cuts[0])
    for cut in cuts[1:]:
        factor_of = factor_of * one(*cut)
    return factor_of


def normal_values(own_key, shape, deviation, reach, pieces=(), held_as=jnp.bfloat16):
    loudness = steps_of(own_key, shape, pieces, -0.22, 0.18) if pieces else 1.0
    result = jax.random.normal(own_key, shape, jnp.float32) * deviation * loudness
    return jnp.minimum(jnp.maximum(result, -reach), reach).astype(held_as)


def setup_inputs(seed: int = 0) -> dict:
    streams_of = jax.random.split(jax.random.key(seed), 8)
    return {
        "inputs": normal_values(streams_of[0], (TOKENS, D), 1.0, 6.0, ((0, 32),)),
        "out_grad": normal_values(streams_of[1], (TOKENS, D), 0.05, 0.29882812, ((0, 32),)),
        "gate_act": normal_values(streams_of[2], (TOKENS, FF), 1.0, 6.0, ((0, 8), (1, 4))),
        "up_act": normal_values(streams_of[3], (TOKENS, FF), 1.0, 6.0, ((0, 8), (1, 4))),
        "w_down": normal_values(streams_of[4], (FF, D), FF ** -0.5, 0.046875, ((0, 4),)),
        "ranks": draw_ranks(jax.random.fold_in(streams_of[7], 71), 0),
        "token_count": draw_token_count(jax.random.fold_in(streams_of[7], 71), 0),
    }


def basis(length, rank_value):
    index_rows = jnp.arange(length, dtype=jnp.float32)[:, None]
    index_cols = jnp.arange(RMAX, dtype=jnp.float32)[None, :]
    table = jnp.cos(jnp.pi * (2.0 * index_rows + 1.0) * index_cols / (2.0 * length)) * jnp.sqrt(2.0 / length)
    table = jnp.where(index_cols == 0.0, table * jnp.sqrt(0.5), table)
    table = jnp.where(index_cols < rank_value.astype(jnp.float32), table, jnp.zeros_like(table))
    return table.astype(jnp.bfloat16)

def orthonormal(ptrans, rank_value):
    gram = jnp.dot(ptrans, ptrans.T, precision=lax.Precision.HIGHEST)
    unused = jnp.where(jnp.arange(RMAX) < rank_value, 0.0, 1.0).astype(gram.dtype)
    lower = jnp.linalg.cholesky(gram + jnp.diag(unused))
    return lax.linalg.triangular_solve(lower, ptrans, left_side=True, lower=True)

def factors(delta, left, basis_table, rank_value):
    projected = jnp.dot(delta.astype(jnp.float32), basis_table.astype(jnp.float32), preferred_element_type=jnp.float32).astype(jnp.bfloat16)
    ptrans = jnp.dot(projected.T.astype(jnp.float32), left.astype(jnp.float32), preferred_element_type=jnp.float32)
    phat = orthonormal(ptrans, rank_value)
    back = jnp.dot(left.astype(jnp.float32), phat.astype(jnp.bfloat16).T.astype(jnp.float32), preferred_element_type=jnp.float32).astype(jnp.bfloat16)
    qtrans = jnp.dot(back.T.astype(jnp.float32), delta.astype(jnp.float32), preferred_element_type=jnp.float32)
    return (phat, qtrans)

def reference(inputs, out_grad, gate_act, up_act, w_down, ranks, token_count):
    replica_rows = TOK_DEV * N_TENSOR
    row_index = jnp.arange(TOKENS, dtype=jnp.int32)
    limits = jnp.repeat(token_count, replica_rows)
    live_rows = row_index % replica_rows < limits
    masked_grad = jnp.where(live_rows[:, None], out_grad, jnp.zeros_like(out_grad))
    width = FF // N_TENSOR
    basis_narrow_gate = basis(width, ranks[0])
    basis_narrow_up = basis(width, ranks[1])
    basis_model = basis(D, ranks[2])
    results = [[], [], [], [], [], []]
    for shard in range(N_TENSOR):
        lower_col = shard * width
        gate = gate_act[:, lower_col:lower_col + width].astype(jnp.float32)
        upper = up_act[:, lower_col:lower_col + width].astype(jnp.float32)
        weight_rows = w_down[lower_col:lower_col + width]
        hidden_grad = jnp.dot(masked_grad.astype(jnp.float32), weight_rows.T.astype(jnp.float32), preferred_element_type=jnp.float32)
        sigmoid_gate = jax.nn.sigmoid(gate)
        silu_gate = gate * sigmoid_gate
        hidden = (silu_gate * upper).astype(jnp.bfloat16)
        d_gate = (hidden_grad * upper * sigmoid_gate * (1.0 + gate * (1.0 - sigmoid_gate))).astype(jnp.bfloat16)
        d_up = (hidden_grad * silu_gate).astype(jnp.bfloat16)
        ph_gate, qt_gate = factors(d_gate, inputs, basis_narrow_gate, ranks[0])
        ph_up, qt_up = factors(d_up, inputs, basis_narrow_up, ranks[1])
        ph_down, qt_down = factors(masked_grad, hidden, basis_model, ranks[2])
        results[0].append(ph_gate * jnp.sqrt(float(D)))
        results[1].append(qt_gate)
        results[2].append(ph_up * jnp.sqrt(float(D)))
        results[3].append(qt_up)
        results[4].append(ph_down * jnp.sqrt(float(width)))
        results[5].append(qt_down)
    return (jnp.stack(results[0]), jnp.concatenate(results[1], axis=1), jnp.stack(results[2]), jnp.concatenate(results[3], axis=1), jnp.concatenate(results[4], axis=1), jnp.stack(results[5]))
```

```python
import functools

import jax
import jax.numpy as jnp
import ml_dtypes
import numpy as np
from jax import lax
from jax.experimental import pallas as pl
from jax.experimental.pallas import tpu as pltpu
from jax.sharding import PartitionSpec as P

RMAX = 64
BF = jnp.bfloat16
F32 = jnp.float32
MESH = pl.DeviceIdType.MESH
TILE = 512
CHUNK = 16
MIB = 1024 * 1024


def basis(length, rank_value, ranks_total):
    index_rows = jnp.arange(length, dtype=jnp.float32)[:, None]
    index_cols = jnp.arange(ranks_total, dtype=jnp.float32)[None, :]
    table = jnp.cos(jnp.pi * (2.0 * index_rows + 1.0) * index_cols / (2.0 * length)) * jnp.sqrt(
        2.0 / length
    )
    table = jnp.where(index_cols == 0.0, table * jnp.sqrt(0.5), table)
    table = jnp.where(index_cols < rank_value.astype(jnp.float32), table, jnp.zeros_like(table))
    return table.astype(jnp.bfloat16)


def solve_rows(gram, ptrans, rank_value):
    ranks_total = gram.shape[0]
    unused = jnp.where(jnp.arange(ranks_total) < rank_value, 0.0, 1.0).astype(jnp.float32)
    lower = jnp.linalg.cholesky(gram + jnp.diag(unused))
    return lax.linalg.triangular_solve(lower, ptrans, left_side=True, lower=True)


def gram_of(ptrans):
    return jnp.dot(ptrans, ptrans.T, precision=lax.Precision.HIGHEST)


def left_factor(delta, left, basis_table):
    projected = jnp.dot(delta, basis_table, preferred_element_type=jnp.float32).astype(jnp.bfloat16)
    return jnp.dot(projected.T, left, preferred_element_type=jnp.float32)


def right_factor(delta, left, phat):
    back = jnp.dot(left, phat.astype(jnp.bfloat16).T, preferred_element_type=jnp.float32).astype(
        jnp.bfloat16
    )
    return jnp.dot(back.T, delta, preferred_element_type=jnp.float32)


def general_body(inputs, out_grad, gate_act, up_act, w_down, ranks, token_count):
    inputs_full, grad_full = (
        lax.all_gather(inputs, "tensor", axis=0, tiled=True),
        lax.all_gather(out_grad, "tensor", axis=0, tiled=True),
    )
    total_rows = inputs_full.shape[0]
    live_rows = jnp.arange(total_rows, dtype=jnp.int32) < token_count[0]
    grad_full = jnp.where(live_rows[:, None], grad_full, jnp.zeros_like(grad_full))
    width = w_down.shape[0]
    features = w_down.shape[1]
    ranks_total = RMAX
    hidden_grad = lax.dot_general(
        grad_full, w_down, (((1,), (1,)), ((), ())), preferred_element_type=jnp.float32
    )
    gate = gate_act.astype(jnp.float32)
    upper = up_act.astype(jnp.float32)
    sigmoid_gate = jax.nn.sigmoid(gate)
    silu_gate = gate * sigmoid_gate
    hidden = (silu_gate * upper).astype(jnp.bfloat16)
    d_gate = (hidden_grad * upper * sigmoid_gate * (1.0 + gate * (1.0 - sigmoid_gate))).astype(
        jnp.bfloat16
    )
    d_up = (hidden_grad * silu_gate).astype(jnp.bfloat16)
    pt_gate = left_factor(d_gate, inputs_full, basis(width, ranks[0], ranks_total))
    pt_up = left_factor(d_up, inputs_full, basis(width, ranks[1], ranks_total))
    pt_down = left_factor(grad_full, hidden, basis(features, ranks[2], ranks_total))
    sum_gate, sum_up, sum_down = lax.psum((pt_gate, pt_up, pt_down), "dp")
    ph_gate = solve_rows(gram_of(sum_gate), sum_gate, ranks[0])
    ph_up = solve_rows(gram_of(sum_up), sum_up, ranks[1])
    ph_down = solve_rows(gram_of(sum_down), sum_down, ranks[2])
    qt_gate = right_factor(d_gate, inputs_full, ph_gate)
    qt_up = right_factor(d_up, inputs_full, ph_up)
    qt_down = right_factor(grad_full, hidden, ph_down)
    sum_qgate, sum_qup, sum_qdown = lax.psum((qt_gate, qt_up, qt_down), "dp")
    scale_model = jnp.sqrt(jnp.float32(features))
    scale_shard = jnp.sqrt(jnp.float32(width))
    return (
        (ph_gate * scale_model)[None],
        sum_qgate,
        (ph_up * scale_model)[None],
        sum_qup,
        ph_down * scale_shard,
        sum_qdown[None],
    )


def table_of(length):
    rows = np.arange(length, dtype=np.float64)[:, None]
    cols = np.arange(RMAX, dtype=np.float64)[None, :]
    table = np.cos(np.pi * (2.0 * rows + 1.0) * cols / (2.0 * length)) * np.sqrt(2.0 / length)
    table[:, 0] *= np.sqrt(0.5)
    return table.astype(np.float32).astype(ml_dtypes.bfloat16)


def dot(left, right, dims):
    return lax.dot_general(left, right, ((dims[:1], dims[1:]), ((), ())), preferred_element_type=F32)


def columns(index, width):
    return pl.ds(pl.multiple_of(index * width, 128), width)


def front_kernel(
    n, x_hbm, g_hbm, gate_hbm, up_hbm, w_hbm, bw_ref, bm_ref, mask_ref,
    x_full, g_full, hid, d_gate, d_up, pt_a, pt_b,
    w_vmem, gate_v, up_v, acc, proj_a, proj_b,
    load_sem, w_sem, own_sem, send_sem, recv_sem,
):
    me = lax.axis_index("tensor")
    rows = x_hbm.shape[0]
    pieces = rows // CHUNK
    width, features = w_hbm.shape
    tiles = width // TILE

    w_loads = [
        pltpu.make_async_copy(
            w_hbm.at[pl.ds(i * TILE, TILE)], w_vmem.at[pl.ds(i * TILE, TILE)], w_sem.at[i]
        )
        for i in range(tiles)
    ]
    own = []
    for a, (hbm, full) in enumerate(((g_hbm, g_full), (x_hbm, x_full))):
        mine = pl.ds(pl.multiple_of(me * rows, rows), rows)
        own.append(pltpu.make_async_copy(hbm, full.at[mine], own_sem.at[a]))
    loads = [
        pltpu.make_async_copy(gate_hbm, gate_v, load_sem.at[0]),
        pltpu.make_async_copy(up_hbm, up_v, load_sem.at[1]),
    ]

    barrier = pltpu.get_barrier_semaphore()

    @pl.when(me > 0)
    def _():
        pl.semaphore_signal(barrier, inc=1, device_id={"tensor": me - 1}, device_id_type=MESH)

    @pl.when(me < n - 1)
    def _():
        pl.semaphore_signal(barrier, inc=1, device_id={"tensor": me + 1}, device_id_type=MESH)

    inside = jnp.logical_and(me > 0, me < n - 1)

    @pl.when(inside)
    def _():
        pl.semaphore_wait(barrier, 2)

    @pl.when(jnp.logical_not(inside))
    def _():
        pl.semaphore_wait(barrier, 1)

    fulls = (g_full, x_full)
    hbms = (g_hbm, x_hbm)

    def copy(a, side, shard, piece, first):
        place = fulls[a].at[pl.ds(pl.multiple_of(shard * rows + piece * CHUNK, CHUNK), CHUNK)]
        source = place
        if first:
            source = hbms[a].at[pl.ds(pl.multiple_of(piece * CHUNK, CHUNK), CHUNK)]
        return pltpu.make_async_remote_copy(
            src_ref=source,
            dst_ref=place,
            send_sem=send_sem.at[a, side, shard, piece],
            recv_sem=recv_sem.at[a, shard, piece],
            device_id={"tensor": me + 1 if side == 0 else me - 1},
            device_id_type=MESH,
        )

    def step(a, d, piece):
        right, left = me - d, me + d
        if d == 0:
            @pl.when(me < n - 1)
            def _():
                copy(a, 0, me, piece, True).start()

            @pl.when(me > 0)
            def _():
                copy(a, 1, me, piece, True).start()

            return

        @pl.when(right >= 0)
        def _():
            copy(a, 1, right, piece, False).wait_recv()

            @pl.when(me < n - 1)
            def _():
                copy(a, 0, right, piece, False).start()

        @pl.when(left < n)
        def _():
            copy(a, 0, left, piece, False).wait_recv()

            @pl.when(me > 0)
            def _():
                copy(a, 1, left, piece, False).start()

    def each_piece(a, d):
        def run(piece, carry):
            step(a, d, piece)
            return carry

        lax.fori_loop(0, pieces, run, 0)

    each_piece(0, 0)
    for item in own + loads + w_loads:
        item.start()
    for d in range(1, n - 1):
        each_piece(0, d)
    each_piece(1, 0)
    each_piece(0, n - 1)
    for item in own + loads + w_loads:
        item.wait()

    proj_b[...] = (dot(g_full[...], bm_ref[...], (1, 0)) * mask_ref[2:3, :]).astype(BF)
    acc[...] = jnp.zeros_like(acc)

    def tile(i, carry):
        cols = columns(i, TILE)
        taken = pl.ds(pl.multiple_of(i * TILE, TILE), TILE)
        hg = dot(g_full[...], w_vmem[taken, :], (1, 1))
        gate = gate_v[:, cols].astype(F32)
        upper = up_v[:, cols].astype(F32)
        sig = 1.0 / (1.0 + jnp.exp(-gate))
        silu = gate * sig
        hidden = (silu * upper).astype(BF)
        dg = (hg * upper * sig * (1.0 + gate * (1.0 - sig))).astype(BF)
        du = (hg * silu).astype(BF)
        hid[:, cols] = hidden
        d_gate[:, cols] = dg
        d_up[:, cols] = du
        table = bw_ref[taken, :]
        acc[0] += dot(dg, table, (1, 0))
        acc[1] += dot(du, table, (1, 0))
        pt_b[:, cols] = dot(proj_b[...], hidden, (0, 0)).astype(BF)

        @pl.when(jnp.logical_and(i >= 2, i < 2 + pieces))
        def _():
            step(1, 1, i - 2)

        return carry

    lax.fori_loop(0, tiles, tile, 0)
    for d in range(2, n):
        each_piece(1, d)

    for k in range(2):
        proj_a[k] = (acc[k] * mask_ref[k:k + 1, :]).astype(BF)

    def left(i, carry):
        cols = columns(i, TILE)
        block = x_full[:, cols]
        for k in range(2):
            pt_a[k * RMAX:(k + 1) * RMAX, cols] = dot(proj_a[k], block, (0, 0)).astype(BF)
        return carry

    lax.fori_loop(0, features // TILE, left, 0)

    for a in range(2):
        for d in range(n):
            def drain(piece, carry, a=a, d=d):
                @pl.when(jnp.logical_and(me - d >= 0, me < n - 1))
                def _():
                    copy(a, 0, me - d, piece, d == 0).wait_send()

                @pl.when(jnp.logical_and(me + d < n, me > 0))
                def _():
                    copy(a, 1, me + d, piece, d == 0).wait_send()

                return carry

            lax.fori_loop(0, pieces, drain, 0)


def sum_kernel(
    a_ref, b_ref, oa_ref, ob_ref, sib_a, sib_b, mid_a, mid_b, got_a, got_b,
    pair_send, pair_recv, rs_send, rs_recv, ag_send, ag_recv, out_send, out_recv,
):
    me = lax.axis_index("dp")
    core = lax.rem(me, 2)
    chip = me // 2
    sibling = chip * 2 + 1 - core
    others = (3 - chip, chip + 1 - 2 * lax.rem(chip, 2), lax.rem(chip + 2, 4))

    barrier = pltpu.get_barrier_semaphore()
    pl.semaphore_signal(barrier, inc=1, device_id={"dp": sibling}, device_id_type=MESH)
    for other in others:
        pl.semaphore_signal(barrier, inc=1, device_id={"dp": other * 2 + core}, device_id_type=MESH)
    pl.semaphore_wait(barrier, 4)

    def remote(src, dst, send, recv, device):
        return pltpu.make_async_remote_copy(
            src_ref=src, dst_ref=dst, send_sem=send, recv_sem=recv,
            device_id={"dp": device}, device_id_type=MESH,
        )

    arrays = (
        (a_ref, oa_ref, sib_a, mid_a, got_a),
        (b_ref, ob_ref, sib_b, mid_b, got_b),
    )
    started = []
    pairs = []
    for n, (src, out, sib, mid, got) in enumerate(arrays):
        half = src.shape[1] // 2
        item = remote(src.at[:, columns(1 - core, half)], sib, pair_send.at[n], pair_recv.at[n], sibling)
        item.start()
        pairs.append(item)
        started.append(item)
    scattered = []
    for n, (src, out, sib, mid, got) in enumerate(arrays):
        half = src.shape[1] // 2
        part = src.shape[0] // 4
        pairs[n].wait_recv()
        mid[...] = (src[:, columns(core, half)].astype(F32) + sib[...].astype(F32)).astype(BF)
        for k, other in enumerate(others):
            rows = pl.ds(pl.multiple_of(other * part, part), part)
            item = remote(mid.at[rows], got.at[k], rs_send.at[n, k], rs_recv.at[n, k], other * 2 + core)
            item.start()
            scattered.append(item)
            started.append(item)
    gathered = []
    handed = []
    for n, (src, out, sib, mid, got) in enumerate(arrays):
        half = src.shape[1] // 2
        part = src.shape[0] // 4
        rows = pl.ds(pl.multiple_of(chip * part, part), part)
        cols = columns(core, half)
        total = src[rows, cols].astype(F32) + sib[rows, :].astype(F32)
        for k in range(3):
            scattered[3 * n + k].wait_recv()
            total = total + got[k].astype(F32)
        out[rows, cols] = total.astype(BF)
        block = out.at[rows, cols]
        for k, other in enumerate(others):
            item = remote(block, block, ag_send.at[n, k], ag_recv.at[n, k], other * 2 + core)
            item.start()
            gathered.append(item)
            started.append(item)
        item = remote(block, block, out_send.at[n, 3], out_recv.at[n, 3], sibling)
        item.start()
        handed.append(item)
        started.append(item)
    for n, (src, out, sib, mid, got) in enumerate(arrays):
        half = src.shape[1] // 2
        part = src.shape[0] // 4
        for k in (1, 2, 0):
            gathered[3 * n + k].wait_recv()
            block = out.at[pl.ds(pl.multiple_of(others[k] * part, part), part), columns(core, half)]
            item = remote(block, block, out_send.at[n, k], out_recv.at[n, k], sibling)
            item.start()
            handed.append(item)
            started.append(item)
    for item in handed:
        item.wait_recv()
    for item in started:
        item.wait_send()


def dp_sum(a, b, number):
    def half(array):
        return pltpu.VMEM((array.shape[0], array.shape[1] // 2), BF)

    def got(array):
        return pltpu.VMEM((3, array.shape[0] // 4, array.shape[1] // 2), BF)

    dma = pltpu.SemaphoreType.DMA
    return pl.pallas_call(
        sum_kernel,
        out_shape=[jax.ShapeDtypeStruct(a.shape, BF), jax.ShapeDtypeStruct(b.shape, BF)],
        in_specs=[pl.BlockSpec(memory_space=pltpu.VMEM)] * 2,
        out_specs=[pl.BlockSpec(memory_space=pltpu.VMEM)] * 2,
        scratch_shapes=[
            half(a), half(b), half(a), half(b), got(a), got(b),
            dma((2,)), dma((2,)), dma((2, 3)), dma((2, 3)), dma((2, 3)), dma((2, 3)),
            dma((2, 4)), dma((2, 4)),
        ],
        compiler_params=pltpu.CompilerParams(
            collective_id=number, has_side_effects=True, vmem_limit_bytes=32 * MIB
        ),
        name="dp_sum_%d" % number,
    )(a, b)


def inverse_factors(grams):
    size = RMAX
    row = lax.broadcasted_iota(jnp.int32, (size, size), 0)
    col = lax.broadcasted_iota(jnp.int32, (size, size), 1)
    eye = jnp.where(row == col, 1.0, 0.0).astype(F32)
    sub = lax.broadcasted_iota(jnp.int32, (8, 2 * size), 0)
    state = []
    for gram in grams:
        joined = jnp.concatenate([eye, gram], axis=1)
        state.append([joined[8 * b:8 * b + 8] for b in range(size // 8)])
    for k in range(size):
        kb, kr = k // 8, k % 8
        for blocks in state:
            pivot_row = blocks[kb][kr:kr + 1, :]
            inv = lax.rsqrt(pivot_row[:, size + k:size + k + 1])
            scaled = pivot_row * inv
            twice = scaled * inv
            for b in range(kb, size // 8):
                block = blocks[b]
                new = block - block[:, size + k:size + k + 1] * twice
                if b == kb:
                    new = jnp.where(sub > kr, new, jnp.where(sub == kr, scaled, block))
                blocks[b] = new
    return [jnp.concatenate(blocks, axis=0)[:, :size] for blocks in state]


def back_kernel(
    pa_ref, pb_ref, unused_ref, x_hbm, g_hbm, hid_hbm, dg_hbm, du_hbm,
    p_gate, p_up, p_down, qa, qb,
    x_v, g_v, hid_v, dg_v, du_v, pha, phb, split, sem,
):
    loads = [
        pltpu.make_async_copy(src, dst, sem.at[i])
        for i, (src, dst) in enumerate(
            ((x_hbm, x_v), (hid_hbm, hid_v), (g_hbm, g_v), (dg_hbm, dg_v), (du_hbm, du_v))
        )
    ]
    for item in loads:
        item.start()
    features = pa_ref.shape[1]
    width = pb_ref.shape[1]
    size = RMAX
    row = lax.broadcasted_iota(jnp.int32, (size, size), 0)
    col = lax.broadcasted_iota(jnp.int32, (size, size), 1)
    both = dot(pa_ref[...], pa_ref[...], (1, 1))
    grams = [both[:size, :size], both[size:, size:], dot(pb_ref[...], pb_ref[...], (1, 1))]
    for k in range(3):
        grams[k] = grams[k] + jnp.where(row == col, unused_ref[k:k + 1, :], 0.0)
    for k, inverse in enumerate(inverse_factors(grams)):
        high = inverse.astype(BF)
        split[k, 0] = high
        split[k, 1] = (inverse - high.astype(F32)).astype(BF)

    def solve(k, block):
        return dot(split[k, 0], block, (1, 0)) + dot(split[k, 1], block, (1, 0))

    def wide(i, carry):
        cols = columns(i, TILE)
        for k, out in enumerate((p_gate, p_up)):
            ph = solve(k, pa_ref[k * size:(k + 1) * size, cols])
            out[0, :, cols] = ph * np.float32(np.sqrt(features))
            pha[k * size:(k + 1) * size, cols] = ph.astype(BF)
        return carry

    lax.fori_loop(0, features // TILE, wide, 0)

    def narrow(i, carry):
        cols = columns(i, TILE)
        ph = solve(2, pb_ref[:, cols])
        p_down[:, cols] = ph * np.float32(np.sqrt(width))
        phb[:, cols] = ph.astype(BF)
        return carry

    lax.fori_loop(0, width // TILE, narrow, 0)
    for item in loads:
        item.wait()
    back_a = dot(x_v[...], pha[...], (1, 1)).astype(BF)
    back_b = dot(hid_v[...], phb[...], (1, 1)).astype(BF)

    def right(i, carry):
        cols = columns(i, TILE)
        qa[:size, cols] = dot(back_a[:, :size], dg_v[:, cols], (0, 0)).astype(BF)
        qa[size:, cols] = dot(back_a[:, size:], du_v[:, cols], (0, 0)).astype(BF)
        return carry

    lax.fori_loop(0, width // TILE, right, 0)

    def right_down(i, carry):
        cols = columns(i, TILE)
        qb[:, cols] = dot(back_b, g_v[:, cols], (0, 0)).astype(BF)
        return carry

    lax.fori_loop(0, features // TILE, right_down, 0)


def kernel_body(n, inputs, out_grad, gate_act, up_act, w_down, ranks, token_count):
    rows, features = inputs.shape
    width = w_down.shape[0]
    total = rows * n
    tiles = width // TILE
    pieces = rows // CHUNK
    here = lax.axis_index("tensor") * rows + jnp.arange(rows, dtype=jnp.int32)
    masked = jnp.where((here < token_count[0])[:, None], out_grad, jnp.zeros_like(out_grad))
    used = jnp.arange(RMAX)[None, :] < ranks[:, None]
    mask = used.astype(F32)
    unused = 1.0 - mask
    dma = pltpu.SemaphoreType.DMA
    vmem = pl.BlockSpec(memory_space=pltpu.VMEM)
    hbm = pl.BlockSpec(memory_space=pl.ANY)

    def shape(*dims):
        return jax.ShapeDtypeStruct(dims, BF)

    x_full, g_full, hid, d_gate, d_up, pt_a, pt_b = pl.pallas_call(
        functools.partial(front_kernel, n),
        out_shape=[
            shape(total, features), shape(total, features), shape(total, width),
            shape(total, width), shape(total, width), shape(2 * RMAX, features), shape(RMAX, width),
        ],
        in_specs=[hbm] * 5 + [vmem] * 3,
        out_specs=[vmem] * 7,
        scratch_shapes=[
            pltpu.VMEM((width, features), BF),
            pltpu.VMEM((total, width), BF),
            pltpu.VMEM((total, width), BF),
            pltpu.VMEM((2, total, RMAX), F32),
            pltpu.VMEM((2, total, RMAX), BF),
            pltpu.VMEM((total, RMAX), BF),
            dma((2,)), dma((tiles,)), dma((2,)),
            dma((2, 2, n, pieces)), dma((2, n, pieces)),
        ],
        compiler_params=pltpu.CompilerParams(
            collective_id=0, has_side_effects=True, vmem_limit_bytes=60 * MIB
        ),
        name="front",
    )(inputs, masked, gate_act, up_act, w_down, jnp.asarray(table_of(width)),
      jnp.asarray(table_of(features)), mask)

    sum_a, sum_b = dp_sum(pt_a, pt_b, 1)

    p_gate, p_up, p_down, qa, qb = pl.pallas_call(
        back_kernel,
        out_shape=[
            jax.ShapeDtypeStruct((1, RMAX, features), F32),
            jax.ShapeDtypeStruct((1, RMAX, features), F32),
            jax.ShapeDtypeStruct((RMAX, width), F32),
            shape(2 * RMAX, width), shape(RMAX, features),
        ],
        in_specs=[vmem] * 3 + [hbm] * 5,
        out_specs=[vmem] * 5,
        scratch_shapes=[
            pltpu.VMEM((total, features), BF), pltpu.VMEM((total, features), BF),
            pltpu.VMEM((total, width), BF), pltpu.VMEM((total, width), BF),
            pltpu.VMEM((total, width), BF),
            pltpu.VMEM((2 * RMAX, features), BF), pltpu.VMEM((RMAX, width), BF),
            pltpu.VMEM((3, 2, RMAX, RMAX), BF),
            dma((5,)),
        ],
        compiler_params=pltpu.CompilerParams(vmem_limit_bytes=48 * MIB),
        name="back",
    )(sum_a, sum_b, unused, x_full, g_full, hid, d_gate, d_up)

    qa, qb = dp_sum(qa, qb, 2)
    return (
        p_gate, qa[:RMAX].astype(F32), p_up, qa[RMAX:].astype(F32), p_down, qb.astype(F32)[None],
    )


def solution(mesh):
    in_specs = (
        P(("dp", "tensor"), None),
        P(("dp", "tensor"), None),
        P("dp", "tensor"),
        P("dp", "tensor"),
        P("tensor", None),
        P(),
        P("dp"),
    )
    out_specs = (
        P("tensor", None, None),
        P(None, "tensor"),
        P("tensor", None, None),
        P(None, "tensor"),
        P(None, "tensor"),
        P("tensor", None, None),
    )
    body = general_body
    if mesh.shape["dp"] == 8 and mesh.shape["tensor"] == 4:
        body = functools.partial(kernel_body, mesh.shape["tensor"])
    return jax.shard_map(body, mesh=mesh, in_specs=in_specs, out_specs=out_specs, check_vma=False)
```

```python
import functools

import jax
import jax.numpy as jnp
import ml_dtypes
import numpy as np
from jax import lax
from jax.experimental import pallas as pl
from jax.experimental.pallas import tpu as pltpu
from jax.sharding import PartitionSpec as P

RMAX = 64
BF = jnp.bfloat16
F32 = jnp.float32
MESH = pl.DeviceIdType.MESH
TILE = 512
CHUNK = 16
MIB = 1024 * 1024


def basis(length, rank_value, ranks_total):
    index_rows = jnp.arange(length, dtype=jnp.float32)[:, None]
    index_cols = jnp.arange(ranks_total, dtype=jnp.float32)[None, :]
    table = jnp.cos(jnp.pi * (2.0 * index_rows + 1.0) * index_cols / (2.0 * length)) * jnp.sqrt(
        2.0 / length
    )
    table = jnp.where(index_cols == 0.0, table * jnp.sqrt(0.5), table)
    table = jnp.where(index_cols < rank_value.astype(jnp.float32), table, jnp.zeros_like(table))
    return table.astype(jnp.bfloat16)


def solve_rows(gram, ptrans, rank_value):
    ranks_total = gram.shape[0]
    unused = jnp.where(jnp.arange(ranks_total) < rank_value, 0.0, 1.0).astype(jnp.float32)
    lower = jnp.linalg.cholesky(gram + jnp.diag(unused))
    return lax.linalg.triangular_solve(lower, ptrans, left_side=True, lower=True)


def gram_of(ptrans):
    return jnp.dot(ptrans, ptrans.T, precision=lax.Precision.HIGHEST)


def left_factor(delta, left, basis_table):
    projected = jnp.dot(delta, basis_table, preferred_element_type=jnp.float32).astype(jnp.bfloat16)
    return jnp.dot(projected.T, left, preferred_element_type=jnp.float32)


def right_factor(delta, left, phat):
    back = jnp.dot(left, phat.astype(jnp.bfloat16).T, preferred_element_type=jnp.float32).astype(
        jnp.bfloat16
    )
    return jnp.dot(back.T, delta, preferred_element_type=jnp.float32)


def general_body(inputs, out_grad, gate_act, up_act, w_down, ranks, token_count):
    inputs_full, grad_full = (
        lax.all_gather(inputs, "tensor", axis=0, tiled=True),
        lax.all_gather(out_grad, "tensor", axis=0, tiled=True),
    )
    total_rows = inputs_full.shape[0]
    live_rows = jnp.arange(total_rows, dtype=jnp.int32) < token_count[0]
    grad_full = jnp.where(live_rows[:, None], grad_full, jnp.zeros_like(grad_full))
    width = w_down.shape[0]
    features = w_down.shape[1]
    ranks_total = RMAX
    hidden_grad = lax.dot_general(
        grad_full, w_down, (((1,), (1,)), ((), ())), preferred_element_type=jnp.float32
    )
    gate = gate_act.astype(jnp.float32)
    upper = up_act.astype(jnp.float32)
    sigmoid_gate = jax.nn.sigmoid(gate)
    silu_gate = gate * sigmoid_gate
    hidden = (silu_gate * upper).astype(jnp.bfloat16)
    d_gate = (hidden_grad * upper * sigmoid_gate * (1.0 + gate * (1.0 - sigmoid_gate))).astype(
        jnp.bfloat16
    )
    d_up = (hidden_grad * silu_gate).astype(jnp.bfloat16)
    pt_gate = left_factor(d_gate, inputs_full, basis(width, ranks[0], ranks_total))
    pt_up = left_factor(d_up, inputs_full, basis(width, ranks[1], ranks_total))
    pt_down = left_factor(grad_full, hidden, basis(features, ranks[2], ranks_total))
    sum_gate, sum_up, sum_down = lax.psum((pt_gate, pt_up, pt_down), "dp")
    ph_gate = solve_rows(gram_of(sum_gate), sum_gate, ranks[0])
    ph_up = solve_rows(gram_of(sum_up), sum_up, ranks[1])
    ph_down = solve_rows(gram_of(sum_down), sum_down, ranks[2])
    qt_gate = right_factor(d_gate, inputs_full, ph_gate)
    qt_up = right_factor(d_up, inputs_full, ph_up)
    qt_down = right_factor(grad_full, hidden, ph_down)
    sum_qgate, sum_qup, sum_qdown = lax.psum((qt_gate, qt_up, qt_down), "dp")
    scale_model = jnp.sqrt(jnp.float32(features))
    scale_shard = jnp.sqrt(jnp.float32(width))
    return (
        (ph_gate * scale_model)[None],
        sum_qgate,
        (ph_up * scale_model)[None],
        sum_qup,
        ph_down * scale_shard,
        sum_qdown[None],
    )


def table_of(length):
    rows = np.arange(length, dtype=np.float64)[:, None]
    cols = np.arange(RMAX, dtype=np.float64)[None, :]
    table = np.cos(np.pi * (2.0 * rows + 1.0) * cols / (2.0 * length)) * np.sqrt(2.0 / length)
    table[:, 0] *= np.sqrt(0.5)
    return table.astype(np.float32).astype(ml_dtypes.bfloat16)


def dot(left, right, dims):
    return lax.dot_general(left, right, ((dims[:1], dims[1:]), ((), ())), preferred_element_type=F32)


def columns(index, width):
    return pl.ds(pl.multiple_of(index * width, 128), width)


def front_kernel(
    n, x_hbm, g_mine, gate_hbm, up_hbm, w_hbm, bw_ref, bm_ref, ranks_ref, count_ref,
    x_out, g_out, hid_out, d_gate_out, d_up_out, pt_a, pt_b,
    x_full, g_full, hid, d_gate, d_up,
    w_vmem, gate_v, up_v, acc, proj_a, proj_b,
    load_sem, w_sem, own_sem, store_sem, send_sem, recv_sem,
):
    me = lax.axis_index("tensor")
    rows = x_hbm.shape[0]
    pieces = rows // CHUNK
    width, features = w_hbm.shape
    tiles = width // TILE

    w_loads = [
        pltpu.make_async_copy(
            w_hbm.at[pl.ds(i * TILE, TILE)], w_vmem.at[pl.ds(i * TILE, TILE)], w_sem.at[i]
        )
        for i in range(tiles)
    ]
    mine = pl.ds(pl.multiple_of(me * rows, rows), rows)
    own = [pltpu.make_async_copy(x_hbm, x_full.at[mine], own_sem.at[0])]
    stores = [
        pltpu.make_async_copy(src, dst, store_sem.at[i])
        for i, (src, dst) in enumerate(
            ((g_full, g_out), (hid, hid_out), (d_gate, d_gate_out), (d_up, d_up_out), (x_full, x_out))
        )
    ]
    loads = [
        pltpu.make_async_copy(gate_hbm, gate_v, load_sem.at[0]),
        pltpu.make_async_copy(up_hbm, up_v, load_sem.at[1]),
    ]

    barrier = pltpu.get_barrier_semaphore()

    @pl.when(me > 0)
    def _():
        pl.semaphore_signal(barrier, inc=1, device_id={"tensor": me - 1}, device_id_type=MESH)

    @pl.when(me < n - 1)
    def _():
        pl.semaphore_signal(barrier, inc=1, device_id={"tensor": me + 1}, device_id_type=MESH)

    row = me * rows + lax.broadcasted_iota(jnp.int32, g_mine.shape, 0)
    g_full[mine, :] = jnp.where(row < count_ref[0], g_mine[...].astype(F32), 0.0).astype(BF)
    rank_col = lax.broadcasted_iota(jnp.int32, (1, RMAX), 1)
    masks = [jnp.where(rank_col < ranks_ref[k], 1.0, 0.0).astype(F32) for k in range(3)]
    inside = jnp.logical_and(me > 0, me < n - 1)

    @pl.when(inside)
    def _():
        pl.semaphore_wait(barrier, 2)

    @pl.when(jnp.logical_not(inside))
    def _():
        pl.semaphore_wait(barrier, 1)

    fulls = (g_full, x_full)

    def copy(a, side, shard, piece, first):
        place = fulls[a].at[pl.ds(pl.multiple_of(shard * rows + piece * CHUNK, CHUNK), CHUNK)]
        source = place
        if first and a == 1:
            source = x_hbm.at[pl.ds(pl.multiple_of(piece * CHUNK, CHUNK), CHUNK)]
        return pltpu.make_async_remote_copy(
            src_ref=source,
            dst_ref=place,
            send_sem=send_sem.at[a, side, shard, piece],
            recv_sem=recv_sem.at[a, shard, piece],
            device_id={"tensor": me + 1 if side == 0 else me - 1},
            device_id_type=MESH,
        )

    def step(a, d, piece):
        right, left = me - d, me + d
        if d == 0:
            @pl.when(me < n - 1)
            def _():
                copy(a, 0, me, piece, True).start()

            @pl.when(me > 0)
            def _():
                copy(a, 1, me, piece, True).start()

            return

        @pl.when(right >= 0)
        def _():
            copy(a, 1, right, piece, False).wait_recv()

            @pl.when(me < n - 1)
            def _():
                copy(a, 0, right, piece, False).start()

        @pl.when(left < n)
        def _():
            copy(a, 0, left, piece, False).wait_recv()

            @pl.when(me > 0)
            def _():
                copy(a, 1, left, piece, False).start()

    def each_piece(a, d):
        def run(piece, carry):
            step(a, d, piece)
            return carry

        lax.fori_loop(0, pieces, run, 0)

    each_piece(0, 0)
    for item in own + loads + w_loads:
        item.start()
    for d in range(1, n - 1):
        each_piece(0, d)
    each_piece(1, 0)
    each_piece(0, n - 1)
    for item in own + loads + w_loads:
        item.wait()

    stores[0].start()
    proj_b[...] = (dot(g_full[...], bm_ref[...], (1, 0)) * masks[2]).astype(BF)
    acc[...] = jnp.zeros_like(acc)

    def tile(i, carry):
        cols = columns(i, TILE)
        taken = pl.ds(pl.multiple_of(i * TILE, TILE), TILE)
        hg = dot(g_full[...], w_vmem[taken, :], (1, 1))
        gate = gate_v[:, cols].astype(F32)
        upper = up_v[:, cols].astype(F32)
        sig = 1.0 / (1.0 + jnp.exp(-gate))
        silu = gate * sig
        hidden = (silu * upper).astype(BF)
        dg = (hg * upper * sig * (1.0 + gate * (1.0 - sig))).astype(BF)
        du = (hg * silu).astype(BF)
        hid[:, cols] = hidden
        d_gate[:, cols] = dg
        d_up[:, cols] = du
        table = bw_ref[taken, :]
        acc[0] += dot(dg, table, (1, 0))
        acc[1] += dot(du, table, (1, 0))
        pt_b[:, cols] = dot(proj_b[...], hidden, (0, 0)).astype(BF)

        @pl.when(jnp.logical_and(i >= 2, i < 2 + pieces))
        def _():
            step(1, 1, i - 2)

        return carry

    lax.fori_loop(0, tiles, tile, 0)
    for item in stores[1:4]:
        item.start()
    for d in range(2, n):
        each_piece(1, d)
    stores[4].start()

    for k in range(2):
        proj_a[k] = (acc[k] * masks[k]).astype(BF)

    def left(i, carry):
        cols = columns(i, TILE)
        block = x_full[:, cols]
        for k in range(2):
            pt_a[k * RMAX:(k + 1) * RMAX, cols] = dot(proj_a[k], block, (0, 0)).astype(BF)
        return carry

    lax.fori_loop(0, features // TILE, left, 0)

    for a in range(2):
        for d in range(n):
            def drain(piece, carry, a=a, d=d):
                @pl.when(jnp.logical_and(me - d >= 0, me < n - 1))
                def _():
                    copy(a, 0, me - d, piece, d == 0).wait_send()

                @pl.when(jnp.logical_and(me + d < n, me > 0))
                def _():
                    copy(a, 1, me + d, piece, d == 0).wait_send()

                return carry

            lax.fori_loop(0, pieces, drain, 0)
    for item in stores:
        item.wait()


def sum_kernel(
    a_ref, b_ref, oa_ref, ob_ref, sib_a, sib_b, mid_a, mid_b, got_a, got_b,
    pair_send, pair_recv, rs_send, rs_recv, ag_send, ag_recv, out_send, out_recv,
):
    me = lax.axis_index("dp")
    core = lax.rem(me, 2)
    chip = me // 2
    sibling = chip * 2 + 1 - core
    others = (3 - chip, chip + 1 - 2 * lax.rem(chip, 2), lax.rem(chip + 2, 4))

    barrier = pltpu.get_barrier_semaphore()
    pl.semaphore_signal(barrier, inc=1, device_id={"dp": sibling}, device_id_type=MESH)
    for other in others:
        pl.semaphore_signal(barrier, inc=1, device_id={"dp": other * 2 + core}, device_id_type=MESH)
    pl.semaphore_wait(barrier, 4)

    def remote(src, dst, send, recv, device):
        return pltpu.make_async_remote_copy(
            src_ref=src, dst_ref=dst, send_sem=send, recv_sem=recv,
            device_id={"dp": device}, device_id_type=MESH,
        )

    arrays = (
        (a_ref, oa_ref, sib_a, mid_a, got_a),
        (b_ref, ob_ref, sib_b, mid_b, got_b),
    )
    started = []
    pairs = []
    for n, (src, out, sib, mid, got) in enumerate(arrays):
        half = src.shape[1] // 2
        item = remote(src.at[:, columns(1 - core, half)], sib, pair_send.at[n], pair_recv.at[n], sibling)
        item.start()
        pairs.append(item)
        started.append(item)
    scattered = []
    for n, (src, out, sib, mid, got) in enumerate(arrays):
        half = src.shape[1] // 2
        part = src.shape[0] // 4
        pairs[n].wait_recv()
        mid[...] = (src[:, columns(core, half)].astype(F32) + sib[...].astype(F32)).astype(BF)
        for k, other in enumerate(others):
            rows = pl.ds(pl.multiple_of(other * part, part), part)
            item = remote(mid.at[rows], got.at[k], rs_send.at[n, k], rs_recv.at[n, k], other * 2 + core)
            item.start()
            scattered.append(item)
            started.append(item)
    gathered = []
    handed = []
    for n, (src, out, sib, mid, got) in enumerate(arrays):
        half = src.shape[1] // 2
        part = src.shape[0] // 4
        rows = pl.ds(pl.multiple_of(chip * part, part), part)
        cols = columns(core, half)
        total = src[rows, cols].astype(F32) + sib[rows, :].astype(F32)
        for k in range(3):
            scattered[3 * n + k].wait_recv()
            total = total + got[k].astype(F32)
        out[rows, cols] = total.astype(BF)
        block = out.at[rows, cols]
        for k, other in enumerate(others):
            item = remote(block, block, ag_send.at[n, k], ag_recv.at[n, k], other * 2 + core)
            item.start()
            gathered.append(item)
            started.append(item)
        item = remote(block, block, out_send.at[n, 3], out_recv.at[n, 3], sibling)
        item.start()
        handed.append(item)
        started.append(item)
    for n, (src, out, sib, mid, got) in enumerate(arrays):
        half = src.shape[1] // 2
        part = src.shape[0] // 4
        for k in (1, 2, 0):
            gathered[3 * n + k].wait_recv()
            block = out.at[pl.ds(pl.multiple_of(others[k] * part, part), part), columns(core, half)]
            item = remote(block, block, out_send.at[n, k], out_recv.at[n, k], sibling)
            item.start()
            handed.append(item)
            started.append(item)
    for item in handed:
        item.wait_recv()
    for item in started:
        item.wait_send()


def dp_sum(a, b, number):
    def half(array):
        return pltpu.VMEM((array.shape[0], array.shape[1] // 2), BF)

    def got(array):
        return pltpu.VMEM((3, array.shape[0] // 4, array.shape[1] // 2), BF)

    dma = pltpu.SemaphoreType.DMA
    return pl.pallas_call(
        sum_kernel,
        out_shape=[jax.ShapeDtypeStruct(a.shape, BF), jax.ShapeDtypeStruct(b.shape, BF)],
        in_specs=[pl.BlockSpec(memory_space=pltpu.VMEM)] * 2,
        out_specs=[pl.BlockSpec(memory_space=pltpu.VMEM)] * 2,
        scratch_shapes=[
            half(a), half(b), half(a), half(b), got(a), got(b),
            dma((2,)), dma((2,)), dma((2, 3)), dma((2, 3)), dma((2, 3)), dma((2, 3)),
            dma((2, 4)), dma((2, 4)),
        ],
        compiler_params=pltpu.CompilerParams(
            collective_id=number, has_side_effects=True, vmem_limit_bytes=32 * MIB
        ),
        name="dp_sum_%d" % number,
    )(a, b)


def inverse_factors(grams):
    size = RMAX
    row = lax.broadcasted_iota(jnp.int32, (size, size), 0)
    col = lax.broadcasted_iota(jnp.int32, (size, size), 1)
    eye = jnp.where(row == col, 1.0, 0.0).astype(F32)
    sub = lax.broadcasted_iota(jnp.int32, (8, 2 * size), 0)
    state = []
    for gram in grams:
        joined = jnp.concatenate([eye, gram], axis=1)
        state.append([joined[8 * b:8 * b + 8] for b in range(size // 8)])
    for k in range(size):
        kb, kr = k // 8, k % 8
        for blocks in state:
            pivot_row = blocks[kb][kr:kr + 1, :]
            inv = lax.rsqrt(pivot_row[:, size + k:size + k + 1])
            scaled = pivot_row * inv
            twice = scaled * inv
            for b in range(kb, size // 8):
                block = blocks[b]
                new = block - block[:, size + k:size + k + 1] * twice
                if b == kb:
                    new = jnp.where(sub > kr, new, jnp.where(sub == kr, scaled, block))
                blocks[b] = new
    return [jnp.concatenate(blocks, axis=0)[:, :size] for blocks in state]


def back_kernel(
    pa_ref, pb_ref, ranks_ref, x_hbm, g_hbm, hid_hbm, dg_hbm, du_hbm,
    p_gate, p_up, p_down, qa, qb,
    x_v, g_v, hid_v, dg_v, du_v, pha, phb, split, sem,
):
    loads = [
        pltpu.make_async_copy(src, dst, sem.at[i])
        for i, (src, dst) in enumerate(
            ((x_hbm, x_v), (hid_hbm, hid_v), (g_hbm, g_v), (dg_hbm, dg_v), (du_hbm, du_v))
        )
    ]
    for item in loads:
        item.start()
    features = pa_ref.shape[1]
    width = pb_ref.shape[1]
    size = RMAX
    row = lax.broadcasted_iota(jnp.int32, (size, size), 0)
    col = lax.broadcasted_iota(jnp.int32, (size, size), 1)
    both = dot(pa_ref[...], pa_ref[...], (1, 1))
    grams = [both[:size, :size], both[size:, size:], dot(pb_ref[...], pb_ref[...], (1, 1))]
    for k in range(3):
        grams[k] = grams[k] + jnp.where(jnp.logical_and(row == col, col >= ranks_ref[k]), 1.0, 0.0)
    for k, inverse in enumerate(inverse_factors(grams)):
        high = inverse.astype(BF)
        split[k, 0] = high
        split[k, 1] = (inverse - high.astype(F32)).astype(BF)

    def solve(k, block):
        return dot(split[k, 0], block, (1, 0)) + dot(split[k, 1], block, (1, 0))

    def wide(i, carry):
        cols = columns(i, TILE)
        for k, out in enumerate((p_gate, p_up)):
            ph = solve(k, pa_ref[k * size:(k + 1) * size, cols])
            out[0, :, cols] = ph * np.float32(np.sqrt(features))
            pha[k * size:(k + 1) * size, cols] = ph.astype(BF)
        return carry

    lax.fori_loop(0, features // TILE, wide, 0)

    def narrow(i, carry):
        cols = columns(i, TILE)
        ph = solve(2, pb_ref[:, cols])
        p_down[:, cols] = ph * np.float32(np.sqrt(width))
        phb[:, cols] = ph.astype(BF)
        return carry

    lax.fori_loop(0, width // TILE, narrow, 0)
    for item in loads:
        item.wait()
    back_a = dot(x_v[...], pha[...], (1, 1)).astype(BF)
    back_b = dot(hid_v[...], phb[...], (1, 1)).astype(BF)

    def right(i, carry):
        cols = columns(i, TILE)
        qa[:size, cols] = dot(back_a[:, :size], dg_v[:, cols], (0, 0)).astype(BF)
        qa[size:, cols] = dot(back_a[:, size:], du_v[:, cols], (0, 0)).astype(BF)
        return carry

    lax.fori_loop(0, width // TILE, right, 0)

    def right_down(i, carry):
        cols = columns(i, TILE)
        qb[:, cols] = dot(back_b, g_v[:, cols], (0, 0)).astype(BF)
        return carry

    lax.fori_loop(0, features // TILE, right_down, 0)


def kernel_body(n, inputs, out_grad, gate_act, up_act, w_down, ranks, token_count):
    rows, features = inputs.shape
    width = w_down.shape[0]
    total = rows * n
    tiles = width // TILE
    pieces = rows // CHUNK
    dma = pltpu.SemaphoreType.DMA
    vmem = pl.BlockSpec(memory_space=pltpu.VMEM)
    hbm = pl.BlockSpec(memory_space=pl.ANY)
    smem = pl.BlockSpec(memory_space=pltpu.SMEM)

    def shape(*dims):
        return jax.ShapeDtypeStruct(dims, BF)

    x_full, g_full, hid, d_gate, d_up, pt_a, pt_b = pl.pallas_call(
        functools.partial(front_kernel, n),
        out_shape=[
            shape(total, features), shape(total, features), shape(total, width),
            shape(total, width), shape(total, width), shape(2 * RMAX, features), shape(RMAX, width),
        ],
        in_specs=[hbm, vmem] + [hbm] * 3 + [vmem] * 2 + [smem] * 2,
        out_specs=[hbm] * 5 + [vmem] * 2,
        scratch_shapes=[
            pltpu.VMEM((total, features), BF), pltpu.VMEM((total, features), BF),
            pltpu.VMEM((total, width), BF), pltpu.VMEM((total, width), BF),
            pltpu.VMEM((total, width), BF),
            pltpu.VMEM((width, features), BF),
            pltpu.VMEM((total, width), BF),
            pltpu.VMEM((total, width), BF),
            pltpu.VMEM((2, total, RMAX), F32),
            pltpu.VMEM((2, total, RMAX), BF),
            pltpu.VMEM((total, RMAX), BF),
            dma((2,)), dma((tiles,)), dma((1,)), dma((5,)),
            dma((2, 2, n, pieces)), dma((2, n, pieces)),
        ],
        compiler_params=pltpu.CompilerParams(
            collective_id=0, has_side_effects=True, vmem_limit_bytes=60 * MIB
        ),
        name="front",
    )(inputs, out_grad, gate_act, up_act, w_down, jnp.asarray(table_of(width)),
      jnp.asarray(table_of(features)), ranks, token_count)

    sum_a, sum_b = dp_sum(pt_a, pt_b, 1)

    p_gate, p_up, p_down, qa, qb = pl.pallas_call(
        back_kernel,
        out_shape=[
            jax.ShapeDtypeStruct((1, RMAX, features), F32),
            jax.ShapeDtypeStruct((1, RMAX, features), F32),
            jax.ShapeDtypeStruct((RMAX, width), F32),
            shape(2 * RMAX, width), shape(RMAX, features),
        ],
        in_specs=[vmem] * 2 + [smem] + [hbm] * 5,
        out_specs=[vmem] * 5,
        scratch_shapes=[
            pltpu.VMEM((total, features), BF), pltpu.VMEM((total, features), BF),
            pltpu.VMEM((total, width), BF), pltpu.VMEM((total, width), BF),
            pltpu.VMEM((total, width), BF),
            pltpu.VMEM((2 * RMAX, features), BF), pltpu.VMEM((RMAX, width), BF),
            pltpu.VMEM((3, 2, RMAX, RMAX), BF),
            dma((5,)),
        ],
        compiler_params=pltpu.CompilerParams(vmem_limit_bytes=48 * MIB),
        name="back",
    )(sum_a, sum_b, ranks, x_full, g_full, hid, d_gate, d_up)

    qa, qb = dp_sum(qa, qb, 2)
    return (
        p_gate, qa[:RMAX].astype(F32), p_up, qa[RMAX:].astype(F32), p_down, qb.astype(F32)[None],
    )


def solution(mesh):
    in_specs = (
        P(("dp", "tensor"), None),
        P(("dp", "tensor"), None),
        P("dp", "tensor"),
        P("dp", "tensor"),
        P("tensor", None),
        P(),
        P("dp"),
    )
    out_specs = (
        P("tensor", None, None),
        P(None, "tensor"),
        P("tensor", None, None),
        P(None, "tensor"),
        P(None, "tensor"),
        P("tensor", None, None),
    )
    body = general_body
    if mesh.shape["dp"] == 8 and mesh.shape["tensor"] == 4:
        body = functools.partial(kernel_body, mesh.shape["tensor"])
    return jax.shard_map(body, mesh=mesh, in_specs=in_specs, out_specs=out_specs, check_vma=False)
```

```python
import functools

import jax
import jax.numpy as jnp
import ml_dtypes
import numpy as np
from jax import lax
from jax.experimental import pallas as pl
from jax.experimental.pallas import tpu as pltpu
from jax.sharding import PartitionSpec as P

RMAX = 64
BF = jnp.bfloat16
F32 = jnp.float32
MESH = pl.DeviceIdType.MESH
TILE = 512
CHUNK = 16
MIB = 1024 * 1024


def basis(length, rank_value, ranks_total):
    index_rows = jnp.arange(length, dtype=jnp.float32)[:, None]
    index_cols = jnp.arange(ranks_total, dtype=jnp.float32)[None, :]
    table = jnp.cos(jnp.pi * (2.0 * index_rows + 1.0) * index_cols / (2.0 * length)) * jnp.sqrt(
        2.0 / length
    )
    table = jnp.where(index_cols == 0.0, table * jnp.sqrt(0.5), table)
    table = jnp.where(index_cols < rank_value.astype(jnp.float32), table, jnp.zeros_like(table))
    return table.astype(jnp.bfloat16)


def solve_rows(gram, ptrans, rank_value):
    ranks_total = gram.shape[0]
    unused = jnp.where(jnp.arange(ranks_total) < rank_value, 0.0, 1.0).astype(jnp.float32)
    lower = jnp.linalg.cholesky(gram + jnp.diag(unused))
    return lax.linalg.triangular_solve(lower, ptrans, left_side=True, lower=True)


def gram_of(ptrans):
    return jnp.dot(ptrans, ptrans.T, precision=lax.Precision.HIGHEST)


def left_factor(delta, left, basis_table):
    projected = jnp.dot(delta, basis_table, preferred_element_type=jnp.float32).astype(jnp.bfloat16)
    return jnp.dot(projected.T, left, preferred_element_type=jnp.float32)


def right_factor(delta, left, phat):
    back = jnp.dot(left, phat.astype(jnp.bfloat16).T, preferred_element_type=jnp.float32).astype(
        jnp.bfloat16
    )
    return jnp.dot(back.T, delta, preferred_element_type=jnp.float32)


def general_body(inputs, out_grad, gate_act, up_act, w_down, ranks, token_count):
    inputs_full, grad_full = (
        lax.all_gather(inputs, "tensor", axis=0, tiled=True),
        lax.all_gather(out_grad, "tensor", axis=0, tiled=True),
    )
    total_rows = inputs_full.shape[0]
    live_rows = jnp.arange(total_rows, dtype=jnp.int32) < token_count[0]
    grad_full = jnp.where(live_rows[:, None], grad_full, jnp.zeros_like(grad_full))
    width = w_down.shape[0]
    features = w_down.shape[1]
    ranks_total = RMAX
    hidden_grad = lax.dot_general(
        grad_full, w_down, (((1,), (1,)), ((), ())), preferred_element_type=jnp.float32
    )
    gate = gate_act.astype(jnp.float32)
    upper = up_act.astype(jnp.float32)
    sigmoid_gate = jax.nn.sigmoid(gate)
    silu_gate = gate * sigmoid_gate
    hidden = (silu_gate * upper).astype(jnp.bfloat16)
    d_gate = (hidden_grad * upper * sigmoid_gate * (1.0 + gate * (1.0 - sigmoid_gate))).astype(
        jnp.bfloat16
    )
    d_up = (hidden_grad * silu_gate).astype(jnp.bfloat16)
    pt_gate = left_factor(d_gate, inputs_full, basis(width, ranks[0], ranks_total))
    pt_up = left_factor(d_up, inputs_full, basis(width, ranks[1], ranks_total))
    pt_down = left_factor(grad_full, hidden, basis(features, ranks[2], ranks_total))
    sum_gate, sum_up, sum_down = lax.psum((pt_gate, pt_up, pt_down), "dp")
    ph_gate = solve_rows(gram_of(sum_gate), sum_gate, ranks[0])
    ph_up = solve_rows(gram_of(sum_up), sum_up, ranks[1])
    ph_down = solve_rows(gram_of(sum_down), sum_down, ranks[2])
    qt_gate = right_factor(d_gate, inputs_full, ph_gate)
    qt_up = right_factor(d_up, inputs_full, ph_up)
    qt_down = right_factor(grad_full, hidden, ph_down)
    sum_qgate, sum_qup, sum_qdown = lax.psum((qt_gate, qt_up, qt_down), "dp")
    scale_model = jnp.sqrt(jnp.float32(features))
    scale_shard = jnp.sqrt(jnp.float32(width))
    return (
        (ph_gate * scale_model)[None],
        sum_qgate,
        (ph_up * scale_model)[None],
        sum_qup,
        ph_down * scale_shard,
        sum_qdown[None],
    )


def table_of(length):
    rows = np.arange(length, dtype=np.float64)[:, None]
    cols = np.arange(RMAX, dtype=np.float64)[None, :]
    table = np.cos(np.pi * (2.0 * rows + 1.0) * cols / (2.0 * length)) * np.sqrt(2.0 / length)
    table[:, 0] *= np.sqrt(0.5)
    return table.astype(np.float32).astype(ml_dtypes.bfloat16)


def dot(left, right, dims):
    return lax.dot_general(left, right, ((dims[:1], dims[1:]), ((), ())), preferred_element_type=F32)


def columns(index, width):
    return pl.ds(pl.multiple_of(index * width, 128), width)


def front_kernel(
    n, x_hbm, g_mine, gate_hbm, up_hbm, w_hbm, bw_ref, bm_ref, ranks_ref, count_ref,
    x_out, g_out, hid_out, d_gate_out, d_up_out, pt_a, sum_b,
    x_full, g_full, hid, d_gate, d_up,
    w_vmem, gate_v, up_v, acc, proj_a, proj_b, pt_b,
    load_sem, w_sem, own_sem, store_sem, send_sem, recv_sem, *sum_refs,
):
    me = lax.axis_index("tensor")
    rows = x_hbm.shape[0]
    pieces = rows // CHUNK
    width, features = w_hbm.shape
    tiles = width // TILE

    w_loads = [
        pltpu.make_async_copy(
            w_hbm.at[pl.ds(i * TILE, TILE)], w_vmem.at[pl.ds(i * TILE, TILE)], w_sem.at[i]
        )
        for i in range(tiles)
    ]
    mine = pl.ds(pl.multiple_of(me * rows, rows), rows)
    own = [pltpu.make_async_copy(x_hbm, x_full.at[mine], own_sem.at[0])]
    stores = [
        pltpu.make_async_copy(src, dst, store_sem.at[i])
        for i, (src, dst) in enumerate(
            ((g_full, g_out), (hid, hid_out), (d_gate, d_gate_out), (d_up, d_up_out), (x_full, x_out))
        )
    ]
    loads = [
        pltpu.make_async_copy(gate_hbm, gate_v, load_sem.at[0]),
        pltpu.make_async_copy(up_hbm, up_v, load_sem.at[1]),
    ]

    down = DpSum(pt_b, sum_b, *sum_refs)
    barrier = pltpu.get_barrier_semaphore()
    for peer in down.peers():
        pl.semaphore_signal(barrier, inc=1, device_id={"dp": peer}, device_id_type=MESH)

    @pl.when(me > 0)
    def _():
        pl.semaphore_signal(barrier, inc=1, device_id={"tensor": me - 1}, device_id_type=MESH)

    @pl.when(me < n - 1)
    def _():
        pl.semaphore_signal(barrier, inc=1, device_id={"tensor": me + 1}, device_id_type=MESH)

    row = me * rows + lax.broadcasted_iota(jnp.int32, g_mine.shape, 0)
    g_full[mine, :] = jnp.where(row < count_ref[0], g_mine[...].astype(F32), 0.0).astype(BF)
    rank_col = lax.broadcasted_iota(jnp.int32, (1, RMAX), 1)
    masks = [jnp.where(rank_col < ranks_ref[k], 1.0, 0.0).astype(F32) for k in range(3)]
    inside = jnp.logical_and(me > 0, me < n - 1)

    @pl.when(inside)
    def _():
        pl.semaphore_wait(barrier, 6)

    @pl.when(jnp.logical_not(inside))
    def _():
        pl.semaphore_wait(barrier, 5)

    fulls = (g_full, x_full)

    def copy(a, side, shard, piece, first):
        place = fulls[a].at[pl.ds(pl.multiple_of(shard * rows + piece * CHUNK, CHUNK), CHUNK)]
        source = place
        if first and a == 1:
            source = x_hbm.at[pl.ds(pl.multiple_of(piece * CHUNK, CHUNK), CHUNK)]
        return pltpu.make_async_remote_copy(
            src_ref=source,
            dst_ref=place,
            send_sem=send_sem.at[a, side, shard, piece],
            recv_sem=recv_sem.at[a, shard, piece],
            device_id={"tensor": me + 1 if side == 0 else me - 1},
            device_id_type=MESH,
        )

    def step(a, d, piece):
        right, left = me - d, me + d
        if d == 0:
            @pl.when(me < n - 1)
            def _():
                copy(a, 0, me, piece, True).start()

            @pl.when(me > 0)
            def _():
                copy(a, 1, me, piece, True).start()

            return

        @pl.when(right >= 0)
        def _():
            copy(a, 1, right, piece, False).wait_recv()

            @pl.when(me < n - 1)
            def _():
                copy(a, 0, right, piece, False).start()

        @pl.when(left < n)
        def _():
            copy(a, 0, left, piece, False).wait_recv()

            @pl.when(me > 0)
            def _():
                copy(a, 1, left, piece, False).start()

    def each_piece(a, d):
        def run(piece, carry):
            step(a, d, piece)
            return carry

        lax.fori_loop(0, pieces, run, 0)

    each_piece(0, 0)
    for item in own + loads + w_loads:
        item.start()
    for d in range(1, n - 1):
        each_piece(0, d)
    each_piece(1, 0)
    each_piece(0, n - 1)
    for item in own + loads + w_loads:
        item.wait()

    stores[0].start()
    proj_b[...] = (dot(g_full[...], bm_ref[...], (1, 0)) * masks[2]).astype(BF)
    acc[...] = jnp.zeros_like(acc)

    def tile(i, carry):
        cols = columns(i, TILE)
        taken = pl.ds(pl.multiple_of(i * TILE, TILE), TILE)
        hg = dot(g_full[...], w_vmem[taken, :], (1, 1))
        gate = gate_v[:, cols].astype(F32)
        upper = up_v[:, cols].astype(F32)
        sig = 1.0 / (1.0 + jnp.exp(-gate))
        silu = gate * sig
        hidden = (silu * upper).astype(BF)
        dg = (hg * upper * sig * (1.0 + gate * (1.0 - sig))).astype(BF)
        du = (hg * silu).astype(BF)
        hid[:, cols] = hidden
        d_gate[:, cols] = dg
        d_up[:, cols] = du
        table = bw_ref[taken, :]
        acc[0] += dot(dg, table, (1, 0))
        acc[1] += dot(du, table, (1, 0))
        pt_b[:, cols] = dot(proj_b[...], hidden, (0, 0)).astype(BF)

        @pl.when(jnp.logical_and(i >= 2, i < 2 + pieces))
        def _():
            step(1, 1, i - 2)

        return carry

    lax.fori_loop(0, tiles, tile, 0)
    for item in stores[1:4]:
        item.start()
    down.start_pair()
    each_piece(1, n - 2)
    down.start_scatter()
    down.start_gather()
    down.start_hand()
    each_piece(1, n - 1)
    stores[4].start()

    for k in range(2):
        proj_a[k] = (acc[k] * masks[k]).astype(BF)

    def left(i, carry):
        cols = columns(i, TILE)
        block = x_full[:, cols]
        for k in range(2):
            pt_a[k * RMAX:(k + 1) * RMAX, cols] = dot(proj_a[k], block, (0, 0)).astype(BF)
        return carry

    lax.fori_loop(0, features // TILE, left, 0)

    for a in range(2):
        for d in range(n):
            def drain(piece, carry, a=a, d=d):
                @pl.when(jnp.logical_and(me - d >= 0, me < n - 1))
                def _():
                    copy(a, 0, me - d, piece, d == 0).wait_send()

                @pl.when(jnp.logical_and(me + d < n, me > 0))
                def _():
                    copy(a, 1, me + d, piece, d == 0).wait_send()

                return carry

            lax.fori_loop(0, pieces, drain, 0)
    for item in stores:
        item.wait()
    down.finish()


class DpSum:
    def __init__(self, src, out, sib, mid, got, pair, scatter, gather, hand):
        me = lax.axis_index("dp")
        self.core = lax.rem(me, 2)
        self.chip = me // 2
        self.sibling = self.chip * 2 + 1 - self.core
        self.others = (
            3 - self.chip, self.chip + 1 - 2 * lax.rem(self.chip, 2), lax.rem(self.chip + 2, 4)
        )
        self.src, self.out, self.sib, self.mid, self.got = src, out, sib, mid, got
        self.sems = (pair, scatter, gather, hand)
        self.half = src.shape[1] // 2
        self.part = src.shape[0] // 4
        self.cols = columns(self.core, self.half)

    def peers(self):
        return [self.sibling] + [other * 2 + self.core for other in self.others]

    def rows(self, chip):
        return pl.ds(pl.multiple_of(chip * self.part, self.part), self.part)

    def remote(self, src, dst, stage, index, device):
        sems = self.sems[stage]
        return pltpu.make_async_remote_copy(
            src_ref=src, dst_ref=dst, send_sem=sems.at[0, index], recv_sem=sems.at[1, index],
            device_id={"dp": device}, device_id_type=MESH,
        )

    def start_pair(self):
        self.pair = self.remote(
            self.src.at[:, columns(1 - self.core, self.half)], self.sib, 0, 0, self.sibling
        )
        self.pair.start()

    def start_scatter(self):
        self.pair.wait_recv()
        both = self.src[:, self.cols].astype(F32) + self.sib[...].astype(F32)
        self.mid[...] = both.astype(BF)
        self.scattered = []
        for k, other in enumerate(self.others):
            item = self.remote(
                self.mid.at[self.rows(other)], self.got.at[k], 1, k, other * 2 + self.core
            )
            item.start()
            self.scattered.append(item)

    def start_gather(self):
        rows = self.rows(self.chip)
        total = self.src[rows, self.cols].astype(F32) + self.sib[rows, :].astype(F32)
        for k in range(3):
            self.scattered[k].wait_recv()
            total = total + self.got[k].astype(F32)
        self.out[rows, self.cols] = total.astype(BF)
        block = self.out.at[rows, self.cols]
        self.gathered = []
        for k, other in enumerate(self.others):
            item = self.remote(block, block, 2, k, other * 2 + self.core)
            item.start()
            self.gathered.append(item)
        item = self.remote(block, block, 3, 3, self.sibling)
        item.start()
        self.handed = [item]

    def start_hand(self):
        for k in (1, 2, 0):
            self.gathered[k].wait_recv()
            block = self.out.at[self.rows(self.others[k]), self.cols]
            item = self.remote(block, block, 3, k, self.sibling)
            item.start()
            self.handed.append(item)

    def finish(self):
        for item in self.handed:
            item.wait_recv()
        for item in [self.pair] + self.scattered + self.gathered + self.handed:
            item.wait_send()


def sum_scratch(rows, cols):
    dma = pltpu.SemaphoreType.DMA
    return [
        pltpu.VMEM((rows, cols // 2), BF), pltpu.VMEM((rows, cols // 2), BF),
        pltpu.VMEM((3, rows // 4, cols // 2), BF),
        dma((2, 1)), dma((2, 3)), dma((2, 3)), dma((2, 4)),
    ]


def sum_kernel(count, *refs):
    sums = [
        DpSum(refs[n], refs[count + n], *refs[2 * count + 7 * n:2 * count + 7 * n + 7])
        for n in range(count)
    ]
    barrier = pltpu.get_barrier_semaphore()
    peers = sums[0].peers()
    for peer in peers:
        pl.semaphore_signal(barrier, inc=1, device_id={"dp": peer}, device_id_type=MESH)
    pl.semaphore_wait(barrier, len(peers))
    for item in sums:
        item.start_pair()
    for item in sums:
        item.start_scatter()
    for item in sums:
        item.start_gather()
    for item in sums:
        item.start_hand()
    for item in sums:
        item.finish()


def dp_sum(number, *arrays):
    count = len(arrays)
    scratch = []
    for array in arrays:
        scratch += sum_scratch(*array.shape)
    return pl.pallas_call(
        functools.partial(sum_kernel, count),
        out_shape=[jax.ShapeDtypeStruct(array.shape, BF) for array in arrays],
        in_specs=[pl.BlockSpec(memory_space=pltpu.VMEM)] * count,
        out_specs=[pl.BlockSpec(memory_space=pltpu.VMEM)] * count,
        scratch_shapes=scratch,
        compiler_params=pltpu.CompilerParams(
            collective_id=number, has_side_effects=True, vmem_limit_bytes=32 * MIB
        ),
        name="dp_sum_%d" % number,
    )(*arrays)


def inverse_factors(grams):
    size = RMAX
    row = lax.broadcasted_iota(jnp.int32, (size, size), 0)
    col = lax.broadcasted_iota(jnp.int32, (size, size), 1)
    eye = jnp.where(row == col, 1.0, 0.0).astype(F32)
    sub = lax.broadcasted_iota(jnp.int32, (8, 2 * size), 0)
    state = []
    for gram in grams:
        joined = jnp.concatenate([eye, gram], axis=1)
        state.append([joined[8 * b:8 * b + 8] for b in range(size // 8)])
    for k in range(size):
        kb, kr = k // 8, k % 8
        for blocks in state:
            pivot_row = blocks[kb][kr:kr + 1, :]
            inv = lax.rsqrt(pivot_row[:, size + k:size + k + 1])
            scaled = pivot_row * inv
            twice = scaled * inv
            for b in range(kb, size // 8):
                block = blocks[b]
                new = block - block[:, size + k:size + k + 1] * twice
                if b == kb:
                    new = jnp.where(sub > kr, new, jnp.where(sub == kr, scaled, block))
                blocks[b] = new
    return [jnp.concatenate(blocks, axis=0)[:, :size] for blocks in state]


def back_kernel(
    pa_ref, pb_ref, ranks_ref, x_hbm, g_hbm, hid_hbm, dg_hbm, du_hbm,
    p_gate, p_up, p_down, qa, qb,
    x_v, g_v, hid_v, dg_v, du_v, pha, phb, split, sem,
):
    loads = [
        pltpu.make_async_copy(src, dst, sem.at[i])
        for i, (src, dst) in enumerate(
            ((x_hbm, x_v), (hid_hbm, hid_v), (g_hbm, g_v), (dg_hbm, dg_v), (du_hbm, du_v))
        )
    ]
    for item in loads:
        item.start()
    features = pa_ref.shape[1]
    width = pb_ref.shape[1]
    size = RMAX
    row = lax.broadcasted_iota(jnp.int32, (size, size), 0)
    col = lax.broadcasted_iota(jnp.int32, (size, size), 1)
    both = dot(pa_ref[...], pa_ref[...], (1, 1))
    grams = [both[:size, :size], both[size:, size:], dot(pb_ref[...], pb_ref[...], (1, 1))]
    for k in range(3):
        grams[k] = grams[k] + jnp.where(jnp.logical_and(row == col, col >= ranks_ref[k]), 1.0, 0.0)
    for k, inverse in enumerate(inverse_factors(grams)):
        high = inverse.astype(BF)
        split[k, 0] = high
        split[k, 1] = (inverse - high.astype(F32)).astype(BF)

    def solve(k, block):
        return dot(split[k, 0], block, (1, 0)) + dot(split[k, 1], block, (1, 0))

    def wide(i, carry):
        cols = columns(i, TILE)
        for k, out in enumerate((p_gate, p_up)):
            ph = solve(k, pa_ref[k * size:(k + 1) * size, cols])
            out[0, :, cols] = ph * np.float32(np.sqrt(features))
            pha[k * size:(k + 1) * size, cols] = ph.astype(BF)
        return carry

    lax.fori_loop(0, features // TILE, wide, 0)

    def narrow(i, carry):
        cols = columns(i, TILE)
        ph = solve(2, pb_ref[:, cols])
        p_down[:, cols] = ph * np.float32(np.sqrt(width))
        phb[:, cols] = ph.astype(BF)
        return carry

    lax.fori_loop(0, width // TILE, narrow, 0)
    for item in loads:
        item.wait()
    back_a = dot(x_v[...], pha[...], (1, 1)).astype(BF)
    back_b = dot(hid_v[...], phb[...], (1, 1)).astype(BF)

    def right(i, carry):
        cols = columns(i, TILE)
        qa[:size, cols] = dot(back_a[:, :size], dg_v[:, cols], (0, 0)).astype(BF)
        qa[size:, cols] = dot(back_a[:, size:], du_v[:, cols], (0, 0)).astype(BF)
        return carry

    lax.fori_loop(0, width // TILE, right, 0)

    def right_down(i, carry):
        cols = columns(i, TILE)
        qb[:, cols] = dot(back_b, g_v[:, cols], (0, 0)).astype(BF)
        return carry

    lax.fori_loop(0, features // TILE, right_down, 0)


def kernel_body(n, inputs, out_grad, gate_act, up_act, w_down, ranks, token_count):
    rows, features = inputs.shape
    width = w_down.shape[0]
    total = rows * n
    tiles = width // TILE
    pieces = rows // CHUNK
    dma = pltpu.SemaphoreType.DMA
    vmem = pl.BlockSpec(memory_space=pltpu.VMEM)
    hbm = pl.BlockSpec(memory_space=pl.ANY)
    smem = pl.BlockSpec(memory_space=pltpu.SMEM)

    def shape(*dims):
        return jax.ShapeDtypeStruct(dims, BF)

    x_full, g_full, hid, d_gate, d_up, pt_a, sum_b = pl.pallas_call(
        functools.partial(front_kernel, n),
        out_shape=[
            shape(total, features), shape(total, features), shape(total, width),
            shape(total, width), shape(total, width), shape(2 * RMAX, features), shape(RMAX, width),
        ],
        in_specs=[hbm, vmem] + [hbm] * 3 + [vmem] * 2 + [smem] * 2,
        out_specs=[hbm] * 5 + [vmem] * 2,
        scratch_shapes=[
            pltpu.VMEM((total, features), BF), pltpu.VMEM((total, features), BF),
            pltpu.VMEM((total, width), BF), pltpu.VMEM((total, width), BF),
            pltpu.VMEM((total, width), BF),
            pltpu.VMEM((width, features), BF),
            pltpu.VMEM((total, width), BF),
            pltpu.VMEM((total, width), BF),
            pltpu.VMEM((2, total, RMAX), F32),
            pltpu.VMEM((2, total, RMAX), BF),
            pltpu.VMEM((total, RMAX), BF),
            pltpu.VMEM((RMAX, width), BF),
            dma((2,)), dma((tiles,)), dma((1,)), dma((5,)),
            dma((2, 2, n, pieces)), dma((2, n, pieces)),
        ] + sum_scratch(RMAX, width),
        compiler_params=pltpu.CompilerParams(
            collective_id=0, has_side_effects=True, vmem_limit_bytes=60 * MIB
        ),
        name="front",
    )(inputs, out_grad, gate_act, up_act, w_down, jnp.asarray(table_of(width)),
      jnp.asarray(table_of(features)), ranks, token_count)

    sum_a, = dp_sum(1, pt_a)

    p_gate, p_up, p_down, qa, qb = pl.pallas_call(
        back_kernel,
        out_shape=[
            jax.ShapeDtypeStruct((1, RMAX, features), F32),
            jax.ShapeDtypeStruct((1, RMAX, features), F32),
            jax.ShapeDtypeStruct((RMAX, width), F32),
            shape(2 * RMAX, width), shape(RMAX, features),
        ],
        in_specs=[vmem] * 2 + [smem] + [hbm] * 5,
        out_specs=[vmem] * 5,
        scratch_shapes=[
            pltpu.VMEM((total, features), BF), pltpu.VMEM((total, features), BF),
            pltpu.VMEM((total, width), BF), pltpu.VMEM((total, width), BF),
            pltpu.VMEM((total, width), BF),
            pltpu.VMEM((2 * RMAX, features), BF), pltpu.VMEM((RMAX, width), BF),
            pltpu.VMEM((3, 2, RMAX, RMAX), BF),
            dma((5,)),
        ],
        compiler_params=pltpu.CompilerParams(vmem_limit_bytes=48 * MIB),
        name="back",
    )(sum_a, sum_b, ranks, x_full, g_full, hid, d_gate, d_up)

    qa, qb = dp_sum(2, qa, qb)
    return (
        p_gate, qa[:RMAX].astype(F32), p_up, qa[RMAX:].astype(F32), p_down, qb.astype(F32)[None],
    )


def solution(mesh):
    in_specs = (
        P(("dp", "tensor"), None),
        P(("dp", "tensor"), None),
        P("dp", "tensor"),
        P("dp", "tensor"),
        P("tensor", None),
        P(),
        P("dp"),
    )
    out_specs = (
        P("tensor", None, None),
        P(None, "tensor"),
        P("tensor", None, None),
        P(None, "tensor"),
        P(None, "tensor"),
        P("tensor", None, None),
    )
    body = general_body
    if mesh.shape["dp"] == 8 and mesh.shape["tensor"] == 4:
        body = functools.partial(kernel_body, mesh.shape["tensor"])
    return jax.shard_map(body, mesh=mesh, in_specs=in_specs, out_specs=out_specs, check_vma=False)
```

```python
import functools

import jax
import jax.numpy as jnp
import ml_dtypes
import numpy as np
from jax import lax
from jax.experimental import pallas as pl
from jax.experimental.pallas import tpu as pltpu
from jax.sharding import PartitionSpec as P

RMAX = 64
BF = jnp.bfloat16
F32 = jnp.float32
MESH = pl.DeviceIdType.MESH
TILE = 512
CHUNK = 16
MIB = 1024 * 1024


def basis(length, rank_value, ranks_total):
    index_rows = jnp.arange(length, dtype=jnp.float32)[:, None]
    index_cols = jnp.arange(ranks_total, dtype=jnp.float32)[None, :]
    table = jnp.cos(jnp.pi * (2.0 * index_rows + 1.0) * index_cols / (2.0 * length)) * jnp.sqrt(
        2.0 / length
    )
    table = jnp.where(index_cols == 0.0, table * jnp.sqrt(0.5), table)
    table = jnp.where(index_cols < rank_value.astype(jnp.float32), table, jnp.zeros_like(table))
    return table.astype(jnp.bfloat16)


def solve_rows(gram, ptrans, rank_value):
    ranks_total = gram.shape[0]
    unused = jnp.where(jnp.arange(ranks_total) < rank_value, 0.0, 1.0).astype(jnp.float32)
    lower = jnp.linalg.cholesky(gram + jnp.diag(unused))
    return lax.linalg.triangular_solve(lower, ptrans, left_side=True, lower=True)


def gram_of(ptrans):
    return jnp.dot(ptrans, ptrans.T, precision=lax.Precision.HIGHEST)


def left_factor(delta, left, basis_table):
    projected = jnp.dot(delta, basis_table, preferred_element_type=jnp.float32).astype(jnp.bfloat16)
    return jnp.dot(projected.T, left, preferred_element_type=jnp.float32)


def right_factor(delta, left, phat):
    back = jnp.dot(left, phat.astype(jnp.bfloat16).T, preferred_element_type=jnp.float32).astype(
        jnp.bfloat16
    )
    return jnp.dot(back.T, delta, preferred_element_type=jnp.float32)


def general_body(inputs, out_grad, gate_act, up_act, w_down, ranks, token_count):
    inputs_full, grad_full = (
        lax.all_gather(inputs, "tensor", axis=0, tiled=True),
        lax.all_gather(out_grad, "tensor", axis=0, tiled=True),
    )
    total_rows = inputs_full.shape[0]
    live_rows = jnp.arange(total_rows, dtype=jnp.int32) < token_count[0]
    grad_full = jnp.where(live_rows[:, None], grad_full, jnp.zeros_like(grad_full))
    width = w_down.shape[0]
    features = w_down.shape[1]
    ranks_total = RMAX
    hidden_grad = lax.dot_general(
        grad_full, w_down, (((1,), (1,)), ((), ())), preferred_element_type=jnp.float32
    )
    gate = gate_act.astype(jnp.float32)
    upper = up_act.astype(jnp.float32)
    sigmoid_gate = jax.nn.sigmoid(gate)
    silu_gate = gate * sigmoid_gate
    hidden = (silu_gate * upper).astype(jnp.bfloat16)
    d_gate = (hidden_grad * upper * sigmoid_gate * (1.0 + gate * (1.0 - sigmoid_gate))).astype(
        jnp.bfloat16
    )
    d_up = (hidden_grad * silu_gate).astype(jnp.bfloat16)
    pt_gate = left_factor(d_gate, inputs_full, basis(width, ranks[0], ranks_total))
    pt_up = left_factor(d_up, inputs_full, basis(width, ranks[1], ranks_total))
    pt_down = left_factor(grad_full, hidden, basis(features, ranks[2], ranks_total))
    sum_gate, sum_up, sum_down = lax.psum((pt_gate, pt_up, pt_down), "dp")
    ph_gate = solve_rows(gram_of(sum_gate), sum_gate, ranks[0])
    ph_up = solve_rows(gram_of(sum_up), sum_up, ranks[1])
    ph_down = solve_rows(gram_of(sum_down), sum_down, ranks[2])
    qt_gate = right_factor(d_gate, inputs_full, ph_gate)
    qt_up = right_factor(d_up, inputs_full, ph_up)
    qt_down = right_factor(grad_full, hidden, ph_down)
    sum_qgate, sum_qup, sum_qdown = lax.psum((qt_gate, qt_up, qt_down), "dp")
    scale_model = jnp.sqrt(jnp.float32(features))
    scale_shard = jnp.sqrt(jnp.float32(width))
    return (
        (ph_gate * scale_model)[None],
        sum_qgate,
        (ph_up * scale_model)[None],
        sum_qup,
        ph_down * scale_shard,
        sum_qdown[None],
    )


def table_of(length):
    rows = np.arange(length, dtype=np.float64)[:, None]
    cols = np.arange(RMAX, dtype=np.float64)[None, :]
    table = np.cos(np.pi * (2.0 * rows + 1.0) * cols / (2.0 * length)) * np.sqrt(2.0 / length)
    table[:, 0] *= np.sqrt(0.5)
    return table.astype(np.float32).astype(ml_dtypes.bfloat16)


def dot(left, right, dims):
    return lax.dot_general(left, right, ((dims[:1], dims[1:]), ((), ())), preferred_element_type=F32)


def columns(index, width):
    return pl.ds(pl.multiple_of(index * width, 128), width)


def front_kernel(
    n, x_hbm, g_mine, gate_hbm, up_hbm, w_hbm, bw_ref, bm_ref, ranks_ref, count_ref,
    x_out, g_out, hid_out, d_gate_out, d_up_out, pt_a, sum_b,
    x_full, g_full, hid, d_gate, d_up,
    w_vmem, gate_v, up_v, acc, proj_a, proj_b, pt_b,
    load_sem, w_sem, own_sem, store_sem, send_sem, recv_sem, *sum_refs,
):
    me = lax.axis_index("tensor")
    rows = x_hbm.shape[0]
    pieces = rows // CHUNK
    width, features = w_hbm.shape
    tiles = width // TILE

    w_loads = [
        pltpu.make_async_copy(
            w_hbm.at[pl.ds(i * TILE, TILE)], w_vmem.at[pl.ds(i * TILE, TILE)], w_sem.at[i]
        )
        for i in range(tiles)
    ]
    mine = pl.ds(pl.multiple_of(me * rows, rows), rows)
    own = [pltpu.make_async_copy(x_hbm, x_full.at[mine], own_sem.at[0])]
    stores = [
        pltpu.make_async_copy(src, dst, store_sem.at[i])
        for i, (src, dst) in enumerate(
            ((g_full, g_out), (hid, hid_out), (d_gate, d_gate_out), (d_up, d_up_out), (x_full, x_out))
        )
    ]
    loads = [
        pltpu.make_async_copy(gate_hbm, gate_v, load_sem.at[0]),
        pltpu.make_async_copy(up_hbm, up_v, load_sem.at[1]),
    ]

    down = DpSum(pt_b, sum_b, *sum_refs)
    barrier = pltpu.get_barrier_semaphore()
    for peer in down.peers():
        pl.semaphore_signal(barrier, inc=1, device_id={"dp": peer}, device_id_type=MESH)

    @pl.when(me > 0)
    def _():
        pl.semaphore_signal(barrier, inc=1, device_id={"tensor": me - 1}, device_id_type=MESH)

    @pl.when(me < n - 1)
    def _():
        pl.semaphore_signal(barrier, inc=1, device_id={"tensor": me + 1}, device_id_type=MESH)

    row = me * rows + lax.broadcasted_iota(jnp.int32, g_mine.shape, 0)
    g_full[mine, :] = jnp.where(row < count_ref[0], g_mine[...].astype(F32), 0.0).astype(BF)
    rank_col = lax.broadcasted_iota(jnp.int32, (1, RMAX), 1)
    masks = [jnp.where(rank_col < ranks_ref[k], 1.0, 0.0).astype(F32) for k in range(3)]
    inside = jnp.logical_and(me > 0, me < n - 1)

    @pl.when(inside)
    def _():
        pl.semaphore_wait(barrier, 6)

    @pl.when(jnp.logical_not(inside))
    def _():
        pl.semaphore_wait(barrier, 5)

    fulls = (g_full, x_full)

    def copy(a, side, shard, piece, first):
        place = fulls[a].at[pl.ds(pl.multiple_of(shard * rows + piece * CHUNK, CHUNK), CHUNK)]
        source = place
        if first and a == 1:
            source = x_hbm.at[pl.ds(pl.multiple_of(piece * CHUNK, CHUNK), CHUNK)]
        return pltpu.make_async_remote_copy(
            src_ref=source,
            dst_ref=place,
            send_sem=send_sem.at[a, side, shard, piece],
            recv_sem=recv_sem.at[a, shard, piece],
            device_id={"tensor": me + 1 if side == 0 else me - 1},
            device_id_type=MESH,
        )

    def step(a, d, piece):
        right, left = me - d, me + d
        if d == 0:
            @pl.when(me < n - 1)
            def _():
                copy(a, 0, me, piece, True).start()

            @pl.when(me > 0)
            def _():
                copy(a, 1, me, piece, True).start()

            return

        @pl.when(right >= 0)
        def _():
            copy(a, 1, right, piece, False).wait_recv()

            @pl.when(me < n - 1)
            def _():
                copy(a, 0, right, piece, False).start()

        @pl.when(left < n)
        def _():
            copy(a, 0, left, piece, False).wait_recv()

            @pl.when(me > 0)
            def _():
                copy(a, 1, left, piece, False).start()

    def each_piece(a, d):
        def run(piece, carry):
            step(a, d, piece)
            return carry

        lax.fori_loop(0, pieces, run, 0)

    each_piece(0, 0)
    for item in own + loads + w_loads:
        item.start()
    for d in range(1, n - 1):
        each_piece(0, d)
    each_piece(1, 0)
    each_piece(0, n - 1)
    for item in own + loads + w_loads:
        item.wait()

    stores[0].start()
    proj_b[...] = (dot(g_full[...], bm_ref[...], (1, 0)) * masks[2]).astype(BF)
    acc[...] = jnp.zeros_like(acc)

    def tile(i, carry):
        cols = columns(i, TILE)
        taken = pl.ds(pl.multiple_of(i * TILE, TILE), TILE)
        hg = dot(g_full[...], w_vmem[taken, :], (1, 1))
        gate = gate_v[:, cols].astype(F32)
        upper = up_v[:, cols].astype(F32)
        sig = 1.0 / (1.0 + jnp.exp(-gate))
        silu = gate * sig
        hidden = (silu * upper).astype(BF)
        dg = (hg * upper * sig * (1.0 + gate * (1.0 - sig))).astype(BF)
        du = (hg * silu).astype(BF)
        hid[:, cols] = hidden
        d_gate[:, cols] = dg
        d_up[:, cols] = du
        table = bw_ref[taken, :]
        acc[0] += dot(dg, table, (1, 0))
        acc[1] += dot(du, table, (1, 0))
        pt_b[:, cols] = dot(proj_b[...], hidden, (0, 0)).astype(BF)

        @pl.when(jnp.logical_and(i >= 2, i < 2 + pieces))
        def _():
            step(1, 1, i - 2)

        return carry

    lax.fori_loop(0, tiles, tile, 0)
    for item in stores[1:4]:
        item.start()
    down.start_pair()
    each_piece(1, n - 2)
    down.start_scatter()
    down.start_gather()
    down.start_hand()
    each_piece(1, n - 1)
    stores[4].start()

    for k in range(2):
        proj_a[k] = (acc[k] * masks[k]).astype(BF)

    def left(i, carry):
        cols = columns(i, TILE)
        block = x_full[:, cols]
        for k in range(2):
            pt_a[k * RMAX:(k + 1) * RMAX, cols] = dot(proj_a[k], block, (0, 0)).astype(BF)
        return carry

    lax.fori_loop(0, features // TILE, left, 0)

    for a in range(2):
        for d in range(n):
            def drain(piece, carry, a=a, d=d):
                @pl.when(jnp.logical_and(me - d >= 0, me < n - 1))
                def _():
                    copy(a, 0, me - d, piece, d == 0).wait_send()

                @pl.when(jnp.logical_and(me + d < n, me > 0))
                def _():
                    copy(a, 1, me + d, piece, d == 0).wait_send()

                return carry

            lax.fori_loop(0, pieces, drain, 0)
    for item in stores:
        item.wait()
    down.finish()


class DpSum:
    def __init__(self, src, out, sib, mid, got, pair, scatter, gather, hand):
        me = lax.axis_index("dp")
        self.core = lax.rem(me, 2)
        self.chip = me // 2
        self.sibling = self.chip * 2 + 1 - self.core
        self.others = (
            3 - self.chip, self.chip + 1 - 2 * lax.rem(self.chip, 2), lax.rem(self.chip + 2, 4)
        )
        self.src, self.out, self.sib, self.mid, self.got = src, out, sib, mid, got
        self.sems = (pair, scatter, gather, hand)
        self.half = src.shape[1] // 2
        self.part = src.shape[0] // 4
        self.cols = columns(self.core, self.half)

    def peers(self):
        return [self.sibling] + [other * 2 + self.core for other in self.others]

    def rows(self, chip):
        return pl.ds(pl.multiple_of(chip * self.part, self.part), self.part)

    def remote(self, src, dst, stage, index, device):
        sems = self.sems[stage]
        return pltpu.make_async_remote_copy(
            src_ref=src, dst_ref=dst, send_sem=sems.at[0, index], recv_sem=sems.at[1, index],
            device_id={"dp": device}, device_id_type=MESH,
        )

    def start_pair(self):
        self.pair = self.remote(
            self.src.at[:, columns(1 - self.core, self.half)], self.sib, 0, 0, self.sibling
        )
        self.pair.start()

    def start_scatter(self):
        self.pair.wait_recv()
        both = self.src[:, self.cols].astype(F32) + self.sib[...].astype(F32)
        self.mid[...] = both.astype(BF)
        self.scattered = []
        for k, other in enumerate(self.others):
            item = self.remote(
                self.mid.at[self.rows(other)], self.got.at[k], 1, k, other * 2 + self.core
            )
            item.start()
            self.scattered.append(item)

    def start_gather(self):
        rows = self.rows(self.chip)
        total = self.src[rows, self.cols].astype(F32) + self.sib[rows, :].astype(F32)
        for k in range(3):
            self.scattered[k].wait_recv()
            total = total + self.got[k].astype(F32)
        self.out[rows, self.cols] = total.astype(BF)
        block = self.out.at[rows, self.cols]
        self.gathered = []
        for k, other in enumerate(self.others):
            item = self.remote(block, block, 2, k, other * 2 + self.core)
            item.start()
            self.gathered.append(item)
        item = self.remote(block, block, 3, 3, self.sibling)
        item.start()
        self.handed = [item]

    def start_hand(self):
        for k in (1, 2, 0):
            self.gathered[k].wait_recv()
            block = self.out.at[self.rows(self.others[k]), self.cols]
            item = self.remote(block, block, 3, k, self.sibling)
            item.start()
            self.handed.append(item)

    def finish(self):
        for item in self.handed:
            item.wait_recv()
        for item in [self.pair] + self.scattered + self.gathered + self.handed:
            item.wait_send()


def sum_scratch(rows, cols):
    dma = pltpu.SemaphoreType.DMA
    return [
        pltpu.VMEM((rows, cols // 2), BF), pltpu.VMEM((rows, cols // 2), BF),
        pltpu.VMEM((3, rows // 4, cols // 2), BF),
        dma((2, 1)), dma((2, 3)), dma((2, 3)), dma((2, 4)),
    ]


def sum_kernel(count, *refs):
    sums = []
    for n in range(count):
        for first in range(0, refs[n].shape[0], RMAX):
            own = 2 * count + 7 * len(sums)
            taken = pl.ds(first, RMAX)
            sums.append(DpSum(refs[n].at[taken], refs[count + n].at[taken], *refs[own:own + 7]))
    barrier = pltpu.get_barrier_semaphore()
    peers = sums[0].peers()
    for peer in peers:
        pl.semaphore_signal(barrier, inc=1, device_id={"dp": peer}, device_id_type=MESH)
    pl.semaphore_wait(barrier, len(peers))
    for item in sums:
        item.start_pair()
    for item in sums:
        item.start_scatter()
    for item in sums:
        item.start_gather()
    for item in sums:
        item.start_hand()
    for item in sums:
        item.finish()


def dp_sum(number, *arrays):
    count = len(arrays)
    scratch = []
    for array in arrays:
        scratch += (array.shape[0] // RMAX) * sum_scratch(RMAX, array.shape[1])
    return pl.pallas_call(
        functools.partial(sum_kernel, count),
        out_shape=[jax.ShapeDtypeStruct(array.shape, BF) for array in arrays],
        in_specs=[pl.BlockSpec(memory_space=pltpu.VMEM)] * count,
        out_specs=[pl.BlockSpec(memory_space=pltpu.VMEM)] * count,
        scratch_shapes=scratch,
        compiler_params=pltpu.CompilerParams(
            collective_id=number, has_side_effects=True, vmem_limit_bytes=32 * MIB
        ),
        name="dp_sum_%d" % number,
    )(*arrays)


def inverse_factors(grams):
    size = RMAX
    row = lax.broadcasted_iota(jnp.int32, (size, size), 0)
    col = lax.broadcasted_iota(jnp.int32, (size, size), 1)
    eye = jnp.where(row == col, 1.0, 0.0).astype(F32)
    sub = lax.broadcasted_iota(jnp.int32, (8, 2 * size), 0)
    state = []
    for gram in grams:
        joined = jnp.concatenate([eye, gram], axis=1)
        state.append([joined[8 * b:8 * b + 8] for b in range(size // 8)])
    for k in range(size):
        kb, kr = k // 8, k % 8
        for blocks in state:
            pivot_row = blocks[kb][kr:kr + 1, :]
            inv = lax.rsqrt(pivot_row[:, size + k:size + k + 1])
            scaled = pivot_row * inv
            twice = scaled * inv
            for b in range(kb, size // 8):
                block = blocks[b]
                new = block - block[:, size + k:size + k + 1] * twice
                if b == kb:
                    new = jnp.where(sub > kr, new, jnp.where(sub == kr, scaled, block))
                blocks[b] = new
    return [jnp.concatenate(blocks, axis=0)[:, :size] for blocks in state]


def back_kernel(
    pa_ref, pb_ref, ranks_ref, x_hbm, g_hbm, hid_hbm, dg_hbm, du_hbm,
    p_gate, p_up, p_down, qa, qb,
    x_v, g_v, hid_v, dg_v, du_v, pha, phb, split, sem,
):
    loads = [
        pltpu.make_async_copy(src, dst, sem.at[i])
        for i, (src, dst) in enumerate(
            ((x_hbm, x_v), (hid_hbm, hid_v), (g_hbm, g_v), (dg_hbm, dg_v), (du_hbm, du_v))
        )
    ]
    for item in loads:
        item.start()
    features = pa_ref.shape[1]
    width = pb_ref.shape[1]
    size = RMAX
    row = lax.broadcasted_iota(jnp.int32, (size, size), 0)
    col = lax.broadcasted_iota(jnp.int32, (size, size), 1)
    both = dot(pa_ref[...], pa_ref[...], (1, 1))
    grams = [both[:size, :size], both[size:, size:], dot(pb_ref[...], pb_ref[...], (1, 1))]
    for k in range(3):
        grams[k] = grams[k] + jnp.where(jnp.logical_and(row == col, col >= ranks_ref[k]), 1.0, 0.0)
    for k, inverse in enumerate(inverse_factors(grams)):
        high = inverse.astype(BF)
        split[k, 0] = high
        split[k, 1] = (inverse - high.astype(F32)).astype(BF)

    def solve(k, block):
        return dot(split[k, 0], block, (1, 0)) + dot(split[k, 1], block, (1, 0))

    def wide(i, carry):
        cols = columns(i, TILE)
        for k, out in enumerate((p_gate, p_up)):
            ph = solve(k, pa_ref[k * size:(k + 1) * size, cols])
            out[0, :, cols] = ph * np.float32(np.sqrt(features))
            pha[k * size:(k + 1) * size, cols] = ph.astype(BF)
        return carry

    lax.fori_loop(0, features // TILE, wide, 0)

    def narrow(i, carry):
        cols = columns(i, TILE)
        ph = solve(2, pb_ref[:, cols])
        p_down[:, cols] = ph * np.float32(np.sqrt(width))
        phb[:, cols] = ph.astype(BF)
        return carry

    lax.fori_loop(0, width // TILE, narrow, 0)
    for item in loads:
        item.wait()
    back_a = dot(x_v[...], pha[...], (1, 1)).astype(BF)
    back_b = dot(hid_v[...], phb[...], (1, 1)).astype(BF)

    def right(i, carry):
        cols = columns(i, TILE)
        qa[:size, cols] = dot(back_a[:, :size], dg_v[:, cols], (0, 0)).astype(BF)
        qa[size:, cols] = dot(back_a[:, size:], du_v[:, cols], (0, 0)).astype(BF)
        return carry

    lax.fori_loop(0, width // TILE, right, 0)

    def right_down(i, carry):
        cols = columns(i, TILE)
        qb[:, cols] = dot(back_b, g_v[:, cols], (0, 0)).astype(BF)
        return carry

    lax.fori_loop(0, features // TILE, right_down, 0)


def kernel_body(n, inputs, out_grad, gate_act, up_act, w_down, ranks, token_count):
    rows, features = inputs.shape
    width = w_down.shape[0]
    total = rows * n
    tiles = width // TILE
    pieces = rows // CHUNK
    dma = pltpu.SemaphoreType.DMA
    vmem = pl.BlockSpec(memory_space=pltpu.VMEM)
    hbm = pl.BlockSpec(memory_space=pl.ANY)
    smem = pl.BlockSpec(memory_space=pltpu.SMEM)

    def shape(*dims):
        return jax.ShapeDtypeStruct(dims, BF)

    x_full, g_full, hid, d_gate, d_up, pt_a, sum_b = pl.pallas_call(
        functools.partial(front_kernel, n),
        out_shape=[
            shape(total, features), shape(total, features), shape(total, width),
            shape(total, width), shape(total, width), shape(2 * RMAX, features), shape(RMAX, width),
        ],
        in_specs=[hbm, vmem] + [hbm] * 3 + [vmem] * 2 + [smem] * 2,
        out_specs=[hbm] * 5 + [vmem] * 2,
        scratch_shapes=[
            pltpu.VMEM((total, features), BF), pltpu.VMEM((total, features), BF),
            pltpu.VMEM((total, width), BF), pltpu.VMEM((total, width), BF),
            pltpu.VMEM((total, width), BF),
            pltpu.VMEM((width, features), BF),
            pltpu.VMEM((total, width), BF),
            pltpu.VMEM((total, width), BF),
            pltpu.VMEM((2, total, RMAX), F32),
            pltpu.VMEM((2, total, RMAX), BF),
            pltpu.VMEM((total, RMAX), BF),
            pltpu.VMEM((RMAX, width), BF),
            dma((2,)), dma((tiles,)), dma((1,)), dma((5,)),
            dma((2, 2, n, pieces)), dma((2, n, pieces)),
        ] + sum_scratch(RMAX, width),
        compiler_params=pltpu.CompilerParams(
            collective_id=0, has_side_effects=True, vmem_limit_bytes=60 * MIB
        ),
        name="front",
    )(inputs, out_grad, gate_act, up_act, w_down, jnp.asarray(table_of(width)),
      jnp.asarray(table_of(features)), ranks, token_count)

    sum_a, = dp_sum(1, pt_a)

    p_gate, p_up, p_down, qa, qb = pl.pallas_call(
        back_kernel,
        out_shape=[
            jax.ShapeDtypeStruct((1, RMAX, features), F32),
            jax.ShapeDtypeStruct((1, RMAX, features), F32),
            jax.ShapeDtypeStruct((RMAX, width), F32),
            shape(2 * RMAX, width), shape(RMAX, features),
        ],
        in_specs=[vmem] * 2 + [smem] + [hbm] * 5,
        out_specs=[vmem] * 5,
        scratch_shapes=[
            pltpu.VMEM((total, features), BF), pltpu.VMEM((total, features), BF),
            pltpu.VMEM((total, width), BF), pltpu.VMEM((total, width), BF),
            pltpu.VMEM((total, width), BF),
            pltpu.VMEM((2 * RMAX, features), BF), pltpu.VMEM((RMAX, width), BF),
            pltpu.VMEM((3, 2, RMAX, RMAX), BF),
            dma((5,)),
        ],
        compiler_params=pltpu.CompilerParams(vmem_limit_bytes=48 * MIB),
        name="back",
    )(sum_a, sum_b, ranks, x_full, g_full, hid, d_gate, d_up)

    qa, qb = dp_sum(2, qa, qb)
    return (
        p_gate, qa[:RMAX].astype(F32), p_up, qa[RMAX:].astype(F32), p_down, qb.astype(F32)[None],
    )


def solution(mesh):
    in_specs = (
        P(("dp", "tensor"), None),
        P(("dp", "tensor"), None),
        P("dp", "tensor"),
        P("dp", "tensor"),
        P("tensor", None),
        P(),
        P("dp"),
    )
    out_specs = (
        P("tensor", None, None),
        P(None, "tensor"),
        P("tensor", None, None),
        P(None, "tensor"),
        P(None, "tensor"),
        P("tensor", None, None),
    )
    body = general_body
    if mesh.shape["dp"] == 8 and mesh.shape["tensor"] == 4:
        body = functools.partial(kernel_body, mesh.shape["tensor"])
    return jax.shard_map(body, mesh=mesh, in_specs=in_specs, out_specs=out_specs, check_vma=False)
```
